256 devices in a mesh: slab: 64 (over x, z, core), cam: 4 (over y).
Axes of the slice: x: 4, y: 4, z: 8, core: 2. Of those that a mesh axis runs over, the one named last changes fastest.
Arguments:
- jac_cam: float32 [18, 16384, 128], P(None, ('slab', 'cam')), may hold values from -0.24 to 0.24
- jac_point: float32 [6, 16384, 128], P(None, ('slab', 'cam')), may hold values from -2.7 to 2.7
- point_ids: int32 [16384, 128], P(('slab', 'cam')), may hold values from 0 to 16383
- block_cam: int32 [16384], P(('slab', 'cam')), may hold values from 0 to 3071, as said below
- block_fill: int32 [16384], P(('slab', 'cam')), may hold values from 16 to 128
- rhs: float32 [9, 12288], P(None, ('slab', 'cam'))
Outputs:
- solution: float32 [9, 12288], P(None, ('slab', 'cam'))
- residual: float32 [9, 12288], P(None, ('slab', 'cam'))
The draws below stay inside these ranges and needn't reach their ends.
Inputs may be any that keep to these rules, and one draw needn't show every extreme that they name: `block_cam`: within one device's 64 blocks the camera numbers never fall; each device's first block has camera 0 and its last camera 3072 - 1.
All inputs are finite; a program needn't handle non-finite values.
Results may differ from the reference program's by a relative error of at most 0.0003.
Values sent between devices are 32-bit elements; how exact they have to be, the bound alone decides.
A program may use at most 128 MiB of HBM per device.

```python
import jax
import jax.numpy as jnp
from jax import lax

CAM_PARAMS = 9
BLOCK_OBS = 128
CAM_DEV = 48
BLK_DEV = 64
PTS = 16384
ITERS = 2
CPC = 3072
CAMS = 12288
BLOCKS = 16384
N_SLAB = 64
N_CAM = 4


def draw_block_cam(key, part):
    key = jax.random.fold_in(key, 11)
    devices = N_SLAB * N_CAM
    raw = jax.random.randint(key, (devices, BLK_DEV), 0, CPC, dtype=jnp.int32)
    ordered = jnp.sort(raw, axis=1)
    ordered = ordered.at[:, 0].set(0).at[:, BLK_DEV - 1].set(CPC - 1)
    return ordered.reshape(-1).astype(jnp.int32)


def draw_block_fill(key, part):
    key = jax.random.fold_in(key, 23)
    index = jnp.arange(BLOCKS, dtype=jnp.int32)
    raw = jax.random.randint(key, (BLOCKS,), 16, BLOCK_OBS + 1, dtype=jnp.int32)
    full = jnp.where(index % 11 == 5, 16, raw)
    return jnp.where(index % 7 == 0, BLOCK_OBS, full).astype(jnp.int32)


def draw_rhs(key, part):
    key = jax.random.fold_in(key, 37)
    first = jax.random.fold_in(key, 0)
    place = jnp.arange(CAMS, dtype=jnp.float32) / max(CAMS - 1, 1)
    rise = 1.0 + 2.0 * place
    values = jax.random.normal(first, (9, CAMS), jnp.float32) * rise
    return values.astype(jnp.float32)


def set_ends(result, key, least, high):
    longest = result.shape.index(max(result.shape))
    spots = []
    for shift in (0, 1):
        where = [jax.random.randint(jax.random.fold_in(key, axis), (), 0, length) for axis, length in enumerate(result.shape)]
        where[longest] = (where[longest] + shift) % result.shape[longest]
        spots.append(tuple(where))
    return result.at[spots[0]].set(least).at[spots[1]].set(high)


def steps_of(stream_key, extent, shards, smallest, top_value):
    loudness = 1.0
    for position, blocks in shards:
        heights = jax.random.uniform(jax.random.fold_in(jax.random.fold_in(stream_key, 6), position), (blocks,), jnp.float32, smallest / len(shards), top_value / len(shards))
        loudness = loudness * jnp.repeat(jnp.exp(heights), extent[position] // blocks).reshape((-1,) + (1,) * (len(extent) - 1 - position))
    return loudness


def noise(stream_key, shape, scale, bound, cuts=(), kind=jnp.bfloat16):
    gain = steps_of(stream_key, shape, cuts, -0.22, 0.18) if cuts else 1.0
    entries = jax.random.normal(stream_key, shape, jnp.float32) * scale * gain
    return jnp.minimum(jnp.maximum(entries, -bound), bound).astype(kind)


def setup_inputs(seed: int = 0) -> dict:
    splits = jax.random.split(jax.random.key(seed), 7)
    jac_cam = noise(splits[0], (2 * CAM_PARAMS, BLOCKS, BLOCK_OBS), 0.04, 0.24, ((1, 256),), jnp.float32)
    jac_point = noise(splits[1], (6, BLOCKS, BLOCK_OBS), 0.45, 2.7, ((1, 256),), jnp.float32)
    point_ids = set_ends(jax.random.randint(splits[2], (BLOCKS, BLOCK_OBS), 0, PTS), jax.random.fold_in(splits[2], 1), 0, PTS - 1).astype(jnp.int32)
    block_cam = draw_block_cam(jax.random.fold_in(splits[6], 71), 0)
    block_fill = draw_block_fill(jax.random.fold_in(splits[6], 71), 0)
    rhs = draw_rhs(jax.random.fold_in(splits[6], 71), 0)
    return {"jac_cam": jac_cam, "jac_point": jac_point, "point_ids": point_ids, "block_cam": block_cam, "block_fill": block_fill, "rhs": rhs}


MU = 1.0
LAMBDA = 0.5


def cofactors(vv):
    v00 = vv[0] + MU
    v01 = vv[1]
    v02 = vv[2]
    v11 = vv[3] + MU
    v12 = vv[4]
    v22 = vv[5] + MU
    c00 = v11 * v22 - v12 * v12
    c01 = v02 * v12 - v01 * v22
    c02 = v01 * v12 - v02 * v11
    c11 = v00 * v22 - v02 * v02
    c12 = v01 * v02 - v00 * v12
    c22 = v00 * v11 - v01 * v01
    det = v00 * c00 + v01 * c01 + v02 * c02
    return jnp.stack([c00, c01, c02, c11, c12, c22, det])


def solve_points(cof, q):
    det = cof[6]
    w0 = (cof[0] * q[0] + cof[1] * q[1] + cof[2] * q[2]) / det
    w1 = (cof[1] * q[0] + cof[3] * q[1] + cof[4] * q[2]) / det
    w2 = (cof[2] * q[0] + cof[4] * q[1] + cof[5] * q[2]) / det
    return jnp.stack([w0, w1, w2])


def reference(jac_cam, jac_point, point_ids, block_cam, block_fill, rhs):
    hi = lax.Precision.HIGHEST
    live = (jnp.arange(BLOCK_OBS, dtype=jnp.int32)[None, :] < block_fill[:, None]).astype(jnp.float32)
    shape = (N_SLAB, N_CAM, BLK_DEV, BLOCK_OBS)
    jcam = (jac_cam * live[None]).reshape((2, 9) + shape)
    jpt = (jac_point * live[None]).reshape((2, 3) + shape)
    slab_of = jnp.arange(N_SLAB, dtype=jnp.int32)[:, None, None, None]
    gid = (point_ids.reshape(shape) + slab_of * PTS).reshape(-1).astype(jnp.int32)
    bcam = block_cam.reshape(N_SLAB, N_CAM, BLK_DEV)
    owner = jnp.broadcast_to(jnp.arange(N_CAM, dtype=jnp.int32)[None, :, None], bcam.shape)

    def to_cluster(x):
        return x.reshape(9, N_SLAB, N_CAM, CAM_DEV).transpose(0, 2, 1, 3).reshape(9, N_CAM, CPC)

    def from_cluster(z):
        return z.reshape(9, N_CAM, N_SLAB, CAM_DEV).transpose(0, 2, 1, 3).reshape(9, CAMS)

    pairs = [(0, 0), (0, 1), (0, 2), (1, 1), (1, 2), (2, 2)]
    prods = jnp.stack([jnp.sum(jpt[:, a] * jpt[:, b], axis=0).reshape(-1) for a, b in pairs])
    vv = jnp.zeros((6, N_SLAB * PTS), jnp.float32).at[:, gid].add(prods)
    cof = cofactors(vv)

    diag_blocks = jnp.sum(jcam * jcam, axis=(0, 5))
    diag_cl = jnp.zeros((9, N_CAM, CPC), jnp.float32).at[:, owner, bcam].add(diag_blocks)
    precond = from_cluster(diag_cl) + LAMBDA

    def apply(x):
        xb = to_cluster(x)[:, owner, bcam]
        e = jnp.einsum('rjskbn,jskb->rskbn', jcam, xb, precision=hi)
        t = jnp.einsum('raskbn,rskbn->askbn', jpt, e, precision=hi).reshape(3, -1)
        q = jnp.zeros((3, N_SLAB * PTS), jnp.float32).at[:, gid].add(t)
        w = solve_points(cof, q)
        wo = w[:, gid].reshape((3,) + shape)
        d = e - jnp.einsum('raskbn,askbn->rskbn', jpt, wo, precision=hi)
        zb = jnp.einsum('rjskbn,rskbn->jskb', jcam, d, precision=hi)
        zcl = jnp.zeros((9, N_CAM, CPC), jnp.float32).at[:, owner, bcam].add(zb)
        return from_cluster(zcl) + LAMBDA * x

    solution = jnp.zeros_like(rhs)
    residual = rhs
    z = residual / precond
    direction = z
    rz = jnp.sum(residual * z)
    for step in range(ITERS):
        image = apply(direction)
        alpha = rz / jnp.sum(direction * image)
        solution = solution + alpha * direction
        residual = residual - alpha * image
        z = residual / precond
        new = jnp.sum(residual * z)
        direction = z + (new / rz) * direction
        rz = new
    return solution, residual
```

```python
import jax
import jax.numpy as jnp
from jax import lax
from jax.experimental import pallas as pl
from jax.experimental.pallas import tpu as pltpu
from jax.sharding import PartitionSpec as P

MU = 1.0
LAMBDA = 0.5

MESH = pl.DeviceIdType.MESH
F32 = jnp.float32
BF16 = jnp.bfloat16

BLK = 64
SLOTS = 128
OWN = 48
NZ = 8
NG = 8
NCAM = 4
HI = 256
LO = 64
LQ = LO // NCAM
CHUNK = 256
CHUNKS = BLK * SLOTS // CHUNK
ROWS = 10

NT = (((1,), (1,)), ((), ()))


def dot_nt(a, b):
    return lax.dot_general(a, b, NT, preferred_element_type=F32)


def dot_nn(a, b):
    return lax.dot_general(a, b, (((1,), (0,)), ((), ())), preferred_element_type=F32)


def split2(v):
    hi = v.astype(BF16).astype(F32)
    return hi, v - hi


def split3(v):
    hi, rest = split2(v)
    mid, low = split2(rest)
    return hi, mid, low


def slab_of(x, z, core):
    return x * (NZ * 2) + z * 2 + core


def total(v):
    return jnp.sum(jnp.sum(v, axis=0, keepdims=True), axis=1, keepdims=True)


def kernel(
    jc_ref, jp_ref, pid_ref, cam_ref, fill_ref, rhs_ref, sol_ref, res_ref,
    jcm, jpm, low_b, low_f, high, equal, t_ref, w_obs, e_ref,
    v_part, v_recv, cof, q_part, q_recv, w_full, w_split, xz, xg, sc,
    zs, zr, gs, gr, vs, vr, qs, qr, ws, wr, ss, sr,
):
    slab = lax.axis_index("slab")
    cam = lax.axis_index("cam")
    core = lax.rem(slab, 2)
    z = lax.rem(lax.div(slab, 2), NZ)
    x = lax.div(slab, 2 * NZ)
    g = x * 2 + core
    odd = lax.rem(z, 2)

    def z_peer(d):
        return (slab_of(x, lax.rem(z + d, NZ), core), cam)

    def g_peer(d):
        other = lax.rem(g + d, NG)
        return (slab_of(lax.div(other, 2), z, lax.rem(other, 2)), cam)

    def cam_peer(d):
        return (slab, lax.rem(cam + d, NCAM))

    barrier = pltpu.get_barrier_semaphore()
    for d in range(1, NZ):
        pl.semaphore_signal(barrier, inc=1, device_id=z_peer(d), device_id_type=MESH)
    for d in range(1, NG):
        pl.semaphore_signal(barrier, inc=1, device_id=g_peer(d), device_id_type=MESH)
    for d in range(1, NCAM):
        pl.semaphore_signal(barrier, inc=1, device_id=cam_peer(d), device_id_type=MESH)
    pl.semaphore_wait(barrier, NZ - 1 + NG - 1 + NCAM - 1)

    pending = []

    def remote(src, dst, send, recv, device):
        copy = pltpu.make_async_remote_copy(
            src_ref=src, dst_ref=dst, send_sem=send, recv_sem=recv, device_id=device, device_id_type=MESH
        )
        copy.start()
        pending.append(copy)
        return copy

    def wait_all(copies):
        for copy in copies:
            copy.wait_recv()

    def z_start(m):
        return [
            remote(xz.at[m, z], xz.at[m, z], zs.at[m, d - 1], zr.at[m, d - 1], z_peer(d))
            for d in range(1, NZ)
        ]

    def g_start(m):
        for p in range(NZ // 2):
            xg[m, g, ROWS * p : ROWS * (p + 1), :] = xz[m, 2 * p] + xz[m, 2 * p + 1]
        return [
            remote(xg.at[m, g], xg.at[m, g], gs.at[m, d - 1], gr.at[m, d - 1], g_peer(d))
            for d in range(1, NG)
        ]

    def camera_sums(m, matrix):
        acc = jnp.zeros((128, 48), F32)
        for other in range(NG):
            rows = xg[m, other]
            wide = jnp.concatenate([rows[ROWS * p : ROWS * (p + 1)] for p in range(NZ // 2)], axis=1)
            wide = jnp.concatenate([wide, jnp.zeros((16 - ROWS, 512), F32)], axis=0)
            parts = jnp.concatenate(split3(wide), axis=0).astype(BF16)
            acc = acc + dot_nt(matrix(other), parts)
        return acc[:, 0:16] + acc[:, 16:32] + acc[:, 32:48]

    rhs = rhs_ref[...]
    first = jnp.concatenate([rhs, jnp.zeros((9, 128 - OWN), F32)], axis=1)
    second = jnp.concatenate([jnp.zeros((9, 64), F32), rhs, jnp.zeros((9, 64 - OWN), F32)], axis=1)
    placed = jnp.where(odd == 0, first, second)
    xz[1, z] = jnp.concatenate([placed, jnp.zeros((1, 128), F32)], axis=0)
    rhs_z = z_start(1)

    def column(row):
        wide = jnp.concatenate([row, jnp.zeros((1, 64), F32)], axis=1)
        return jnp.broadcast_to(wide, (128, 128)).T

    cam_col = column(cam_ref[...].astype(F32))
    fill_col = column(fill_ref[...].astype(F32))
    sub = lax.broadcasted_iota(jnp.int32, (128, 128), 0)
    lane = lax.broadcasted_iota(jnp.int32, (128, 128), 1)
    own_cam = (slab * OWN + sub - 64).astype(F32)
    is_own = (sub >= 64) & (sub < 64 + OWN)
    targets = jnp.where(sub < 64, cam_col, jnp.where(is_own, own_cam, -1.0))

    live = (lane.astype(F32) < fill_col)[:BLK]
    for i in range(18):
        jcm[i] = jnp.where(live, jc_ref[i], 0.0)
    for i in range(6):
        jpm[i] = jnp.where(live, jp_ref[i], 0.0)

    lane64 = lane[:BLK]
    sub64 = sub[:BLK]

    def to_message(m, columns):
        padded = jnp.zeros((64, 128), F32)
        both = jnp.where(
            odd == 0,
            jnp.concatenate([columns, padded], axis=0),
            jnp.concatenate([padded, columns], axis=0),
        )
        xz[m, z] = both.T[:ROWS]

    diag = jnp.where(lane64 == 9, cam_col[:BLK], 0.0)
    for j in range(9):
        square = jnp.sum(jcm[j] * jcm[j] + jcm[9 + j] * jcm[9 + j], axis=1, keepdims=True)
        diag = jnp.where(lane64 == j, square, diag)
    to_message(0, diag)
    diag_z = z_start(0)

    def build(k, carry):
        ids = jnp.concatenate([pid_ref[pl.ds(2 * k, 1), :], pid_ref[pl.ds(2 * k + 1, 1), :]], axis=1)
        low = lax.bitwise_and(ids, LO - 1)
        top = lax.shift_right_logical(ids, 6)
        hot = lax.broadcasted_iota(jnp.int32, (HI, CHUNK), 0) == top
        high[k] = jnp.where(hot, 1.0, 0.0).astype(BF16)
        hot_low = jnp.where(lax.broadcasted_iota(jnp.int32, (LO, CHUNK), 0) == low, 1.0, 0.0)
        low_f[k] = hot_low
        low_b[k] = hot_low.astype(BF16)
        return carry

    lax.fori_loop(0, CHUNKS, build, 0)

    wait_all(rhs_z)
    rhs_g = g_start(1)
    wait_all(diag_z)
    diag_g = g_start(0)

    def pair(ref, index, k):
        return jnp.concatenate([ref[index, pl.ds(2 * k, 1), :], ref[index, pl.ds(2 * k + 1, 1), :]], axis=1)

    def scatter(rows_of, count, acc_ref):
        half = NCAM * count * LQ
        acc_ref[...] = jnp.zeros_like(acc_ref)

        def body(k, carry):
            parts = [], []
            for row in rows_of(k):
                for part, value in zip(parts, split2(row)):
                    part.append(jnp.broadcast_to(value, (LQ, CHUNK)).astype(BF16))
            blocks = [
                low_b[k, LQ * q : LQ * (q + 1), :] * value for part in parts for q in range(NCAM) for value in part
            ]
            product = dot_nt(jnp.concatenate(blocks, axis=0), high[k])
            acc_ref[...] += (product[:half] + product[half:]).reshape(NCAM, count * LQ, HI)
            return carry

        lax.fori_loop(0, CHUNKS, body, 0)

    def jp_products(k):
        a = [pair(jpm, i, k) for i in range(6)]
        return [a[i] * a[j] + a[3 + i] * a[3 + j] for i, j in ((0, 0), (0, 1), (0, 2), (1, 1), (1, 2), (2, 2))]

    scatter(jp_products, 6, v_part)
    v_copies = [
        remote(v_part.at[lax.rem(cam + d, NCAM)], v_recv.at[d - 1], vs.at[d - 1], vr.at[d - 1], cam_peer(d))
        for d in range(1, NCAM)
    ]

    wait_all(diag_g)
    for other in range(NG):
        for p in range(NZ // 2):
            ids = xg[0, other, ROWS * p + 9 : ROWS * p + 10, :]
            equal[other, :, 128 * p : 128 * (p + 1)] = jnp.where(targets == ids, 1.0, 0.0).astype(BF16)

    def same(other):
        return equal[other]

    def owned(other):
        lanes = lax.broadcasted_iota(jnp.int32, (1, 128), 1)
        place = lax.rem(lanes, 64)
        blocks = []
        for p in range(NZ // 2):
            source = (other // 2) * (2 * NZ) + (2 * p + lax.div(lanes, 64)) * 2 + other % 2
            ids = jnp.where(place < OWN, source * OWN + place, -2).astype(F32)
            blocks.append(jnp.where(targets == ids, 1.0, 0.0).astype(BF16))
        return jnp.concatenate(blocks, axis=1)

    lane16 = lax.broadcasted_iota(jnp.int32, (128, 16), 1)
    sub16 = lax.broadcasted_iota(jnp.int32, (128, 16), 0)
    param = lane16 < 9
    mine = param & (sub16 >= 64) & (sub16 < 64 + OWN)
    precond = jnp.where(param, camera_sums(0, same), 0.0) + LAMBDA
    wait_all(rhs_g)
    res0 = camera_sums(1, owned)
    dir0 = res0 / precond

    def apply(it, vec, scalars):
        cols = [jnp.broadcast_to(vec[:BLK, j : j + 1], (BLK, SLOTS)) for j in range(9)]
        for r in range(2):
            e = jcm[9 * r] * cols[0]
            for j in range(1, 9):
                e = e + jcm[9 * r + j] * cols[j]
            e_ref[r] = e
        for a in range(3):
            t_ref[a] = jpm[a] * e_ref[0] + jpm[3 + a] * e_ref[1]
        scatter(lambda k: [pair(t_ref, a, k) for a in range(3)], 3, q_part.at[it])
        q_copies = [
            remote(
                q_part.at[it, lax.rem(cam + d, NCAM)], q_recv.at[it, d - 1],
                qs.at[it, d - 1], qr.at[it, d - 1], cam_peer(d),
            )
            for d in range(1, NCAM)
        ]
        if it == 0:
            wait_all(v_copies)
            v = v_part[cam] + v_recv[0] + v_recv[1] + v_recv[2]
            v00, v01, v02, v11, v12, v22 = [v[LQ * i : LQ * (i + 1)] for i in range(6)]
            v00, v11, v22 = v00 + MU, v11 + MU, v22 + MU
            c00 = v11 * v22 - v12 * v12
            c01 = v02 * v12 - v01 * v22
            c02 = v01 * v12 - v02 * v11
            c11 = v00 * v22 - v02 * v02
            c12 = v01 * v02 - v00 * v12
            c22 = v00 * v11 - v01 * v01
            det = v00 * c00 + v01 * c01 + v02 * c02
            for i, value in enumerate((c00, c01, c02, c11, c12, c22)):
                cof[i] = value
            cof[6] = det
        wait_all(q_copies)
        q = q_part[it, cam] + q_recv[it, 0] + q_recv[it, 1] + q_recv[it, 2]
        q0, q1, q2 = [q[LQ * i : LQ * (i + 1)] for i in range(3)]
        det = cof[6]
        w0 = (cof[0] * q0 + cof[1] * q1 + cof[2] * q2) / det
        w1 = (cof[1] * q0 + cof[3] * q1 + cof[4] * q2) / det
        w2 = (cof[2] * q0 + cof[4] * q1 + cof[5] * q2) / det
        w_full[it, cam] = jnp.concatenate([w0, w1, w2], axis=0)
        w_copies = [
            remote(w_full.at[it, cam], w_full.at[it, cam], ws.at[it, d - 1], wr.at[it, d - 1], cam_peer(d))
            for d in range(1, NCAM)
        ]
        wait_all(w_copies)
        half = NCAM * 3 * LQ
        for part, value in enumerate(split2(w_full[it].reshape(half, HI))):
            w_split[half * part : half * (part + 1)] = value.astype(BF16)

        def body(k, carry):
            product = dot_nn(w_split[...], high[k])
            product = product[:half] + product[half:]
            for c in range(3):
                picked = jnp.zeros((LQ, CHUNK), F32)
                for q in range(NCAM):
                    at = (3 * q + c) * LQ
                    picked = picked + product[at : at + LQ] * low_f[k, LQ * q : LQ * (q + 1), :]
                row = jnp.sum(picked, axis=0, keepdims=True)
                w_obs[c, pl.ds(2 * k, 1), :] = row[:, :SLOTS]
                w_obs[c, pl.ds(2 * k + 1, 1), :] = row[:, SLOTS:]
            return carry

        lax.fori_loop(0, CHUNKS, body, 0)
        d = [
            e_ref[r] - (jpm[3 * r] * w_obs[0] + jpm[3 * r + 1] * w_obs[1] + jpm[3 * r + 2] * w_obs[2])
            for r in range(2)
        ]
        terms = jnp.zeros((BLK, 128), F32)
        for j in range(9):
            term = jnp.sum(jcm[j] * d[0] + jcm[9 + j] * d[1], axis=1, keepdims=True)
            terms = jnp.where(lane64 == j, term, terms)
        if scalars is not None:
            known = scalars + [LAMBDA * total(jnp.where(mine, vec * vec, 0.0)) + total(terms[:, :16] * vec[:BLK])]
            for i, value in enumerate(known):
                terms = jnp.where((lane64 == 9) & (sub64 == i), value, terms)
        m = 2 + it
        to_message(m, terms)
        wait_all(z_start(m))
        wait_all(g_start(m))
        return m

    m = apply(0, dir0, None)
    image0 = jnp.where(param, camera_sums(m, same), 0.0) + LAMBDA * dir0
    rest = res0 - image0
    dir1 = rest / precond
    dots = [total(jnp.where(mine, a * b, 0.0)) for a, b in ((res0, dir0), (dir0, rest), (rest, dir1))]
    m = apply(1, dir1, dots)

    row = jnp.zeros((1, 128), F32)
    for other in range(NG):
        for p in range(NZ // 2):
            row = row + xg[m, other, ROWS * p + 9 : ROWS * p + 10, :]
    row = row[:, :64] + row[:, 64:]
    sc[cam] = jnp.concatenate([row, jnp.zeros((1, 64), F32)], axis=1)
    sc_copies = [
        remote(sc.at[cam], sc.at[cam], ss.at[d - 1], sr.at[d - 1], cam_peer(d)) for d in range(1, NCAM)
    ]
    image1 = jnp.where(param, camera_sums(m, same), 0.0) + LAMBDA * dir1
    wait_all(sc_copies)
    sums = sc[0] + sc[1] + sc[2] + sc[3]
    aa, bb, cc, dd = [sums[:, i : i + 1] for i in range(4)]
    curve = aa - bb
    alpha0 = aa / curve
    keep = -bb / curve
    rz1 = keep * keep * aa + 2.0 * keep * alpha0 * bb + alpha0 * alpha0 * cc
    scale = keep + rz1 / aa
    alpha1 = rz1 / (scale * scale * curve + 2.0 * scale * alpha0 * (bb - cc) + alpha0 * alpha0 * dd)
    dir_last = scale * dir0 + alpha0 * dir1
    img_last = scale * image0 + alpha0 * image1
    sol = alpha0 * dir0 + alpha1 * dir_last
    res = keep * res0 + alpha0 * rest - alpha1 * img_last

    def to_rows(value):
        wide = jnp.concatenate([value, jnp.zeros((128, 112), F32)], axis=1)
        return wide.T[:9, 64 : 64 + OWN]

    sol_ref[...] = to_rows(sol)
    res_ref[...] = to_rows(res)
    for copy in pending:
        copy.wait_send()


def local(jac_cam, jac_point, point_ids, block_cam, block_fill, rhs):
    dma = pltpu.SemaphoreType.DMA
    vmem = pl.BlockSpec(memory_space=pltpu.VMEM)
    own = jax.ShapeDtypeStruct((9, OWN), F32)
    return pl.pallas_call(
        kernel,
        out_shape=(own, own),
        in_specs=[vmem] * 6,
        out_specs=(vmem, vmem),
        scratch_shapes=[
            pltpu.VMEM((18, BLK, SLOTS), F32),
            pltpu.VMEM((6, BLK, SLOTS), F32),
            pltpu.VMEM((CHUNKS, LO, CHUNK), BF16),
            pltpu.VMEM((CHUNKS, LO, CHUNK), F32),
            pltpu.VMEM((CHUNKS, HI, CHUNK), BF16),
            pltpu.VMEM((NG, 128, 512), BF16),
            pltpu.VMEM((3, BLK, SLOTS), F32),
            pltpu.VMEM((3, BLK, SLOTS), F32),
            pltpu.VMEM((2, BLK, SLOTS), F32),
            pltpu.VMEM((NCAM, 6 * LQ, HI), F32),
            pltpu.VMEM((NCAM - 1, 6 * LQ, HI), F32),
            pltpu.VMEM((7, LQ, HI), F32),
            pltpu.VMEM((2, NCAM, 3 * LQ, HI), F32),
            pltpu.VMEM((2, NCAM - 1, 3 * LQ, HI), F32),
            pltpu.VMEM((2, NCAM, 3 * LQ, HI), F32),
            pltpu.VMEM((2 * NCAM * 3 * LQ, HI), BF16),
            pltpu.VMEM((4, NZ, ROWS, 128), F32),
            pltpu.VMEM((4, NG, ROWS * NZ // 2, 128), F32),
            pltpu.VMEM((NCAM, 1, 128), F32),
            dma((4, NZ - 1)),
            dma((4, NZ - 1)),
            dma((4, NG - 1)),
            dma((4, NG - 1)),
            dma((NCAM - 1,)),
            dma((NCAM - 1,)),
            dma((2, NCAM - 1)),
            dma((2, NCAM - 1)),
            dma((2, NCAM - 1)),
            dma((2, NCAM - 1)),
            dma((NCAM - 1,)),
            dma((NCAM - 1,)),
        ],
        compiler_params=pltpu.CompilerParams(
            collective_id=0, has_side_effects=True, vmem_limit_bytes=40 * 1024 * 1024
        ),
        name="schur_cg",
    )(jac_cam, jac_point, point_ids, block_cam.reshape(1, BLK), block_fill.reshape(1, BLK), rhs)


def solution(mesh):
    placed = (
        P(None, ("slab", "cam"), None),
        P(None, ("slab", "cam"), None),
        P(("slab", "cam"), None),
        P(("slab", "cam")),
        P(("slab", "cam")),
        P(None, ("slab", "cam")),
    )
    return jax.shard_map(
        local,
        mesh=mesh,
        in_specs=placed,
        out_specs=(P(None, ("slab", "cam")), P(None, ("slab", "cam"))),
        check_vma=False,
    )
```

```python
import jax
import jax.numpy as jnp
from jax import lax
from jax.experimental import pallas as pl
from jax.experimental.pallas import tpu as pltpu
from jax.sharding import PartitionSpec as P

MU = 1.0
LAMBDA = 0.5

MESH = pl.DeviceIdType.MESH
F32 = jnp.float32
BF16 = jnp.bfloat16

BLK = 64
SLOTS = 128
OWN = 48
NX = 4
NZ = 8
NCHIP = NX * NZ
NCAM = 4
HI = 256
LO = 64
LQ = LO // NCAM
CHUNK = 256
CHUNKS = BLK * SLOTS // CHUNK
STEPS = 8
MSG = 5
GROUP = 4

NT = (((1,), (1,)), ((), ()))


def dot_nt(a, b):
    return lax.dot_general(a, b, NT, preferred_element_type=F32)


def dot_nn(a, b):
    return lax.dot_general(a, b, (((1,), (0,)), ((), ())), preferred_element_type=F32)


def split2(v):
    hi = v.astype(BF16).astype(F32)
    return hi, v - hi


def split3(v):
    hi, rest = split2(v)
    mid, low = split2(rest)
    return hi, mid, low


def far_first():
    def hops(offset):
        dx, dz = offset
        return min(dx, NX - dx) + min(dz, NZ - dz)

    offsets = [(dx, dz) for dx in range(NX) for dz in range(NZ) if dx or dz]
    return sorted(offsets, key=hops, reverse=True)


OFFSETS = far_first()


def column_of(j):
    return (j % 2) * 8 + j // 2


def total(v):
    return jnp.sum(jnp.sum(v, axis=0, keepdims=True), axis=1, keepdims=True)


def kernel(
    jc_hbm, jp_hbm, pid_hbm, cam_hbm, fill_hbm, rhs_hbm, sol_ref, res_ref,
    jcm, jpm, pid_ref, cam_ref, fill_ref, rhs_ref, low_b, low_f, high, equal, t_ref, w_obs, e_ref,
    v_part, v_recv, cof, q_part, q_recv, w_full, w_split, first_msg, msgs, sc,
    ins, cs, cr, ps, pr, vs, vr, qs, qr, ws, wr, ss, sr,
):
    slab = lax.axis_index("slab")
    cam = lax.axis_index("cam")
    core = lax.rem(slab, 2)
    z = lax.rem(lax.div(slab, 2), NZ)
    x = lax.div(slab, 2 * NZ)
    chip = x * NZ + z

    def chip_peer(offset):
        dx, dz = offset
        other = lax.rem(x + dx, NX) * NZ + lax.rem(z + dz, NZ)
        return (other * 2 + core, cam)

    sibling = (chip * 2 + (1 - core), cam)

    def cam_peer(d):
        return (slab, lax.rem(cam + d, NCAM))

    inputs = [
        pltpu.make_async_copy(src, dst, ins.at[i])
        for i, (src, dst) in enumerate(
            (
                (fill_hbm, fill_ref), (cam_hbm, cam_ref), (rhs_hbm, rhs_ref),
                (jc_hbm, jcm), (pid_hbm, pid_ref), (jp_hbm, jpm),
            )
        )
    ]
    for copy in inputs:
        copy.start()
    barrier = pltpu.get_barrier_semaphore()
    for offset in OFFSETS:
        pl.semaphore_signal(barrier, inc=1, device_id=chip_peer(offset), device_id_type=MESH)
    for d in range(1, NCAM):
        pl.semaphore_signal(barrier, inc=1, device_id=cam_peer(d), device_id_type=MESH)
    pl.semaphore_signal(barrier, inc=1, device_id=sibling, device_id_type=MESH)

    pending = []

    def remote(src, dst, send, recv, device):
        copy = pltpu.make_async_remote_copy(
            src_ref=src, dst_ref=dst, send_sem=send, recv_sem=recv, device_id=device, device_id_type=MESH
        )
        copy.start()
        pending.append(copy)
        return copy

    def wait_all(copies):
        for copy in copies:
            copy.wait_recv()

    def gather_start(buf, m):
        mine = buf.at[core, chip]
        return [
            remote(mine, mine, cs.at[m, i], cr.at[m, i], chip_peer(offset)) for i, offset in enumerate(OFFSETS)
        ]

    def gather_end(copies, buf, m):
        wait_all(copies)
        remote(buf.at[core], buf.at[core], ps.at[m], pr.at[m], sibling).wait_recv()

    lane8 = lax.broadcasted_iota(jnp.int32, (8, 128), 1)

    def both_cores(zero, one):
        zero, one = [jnp.concatenate([v, jnp.zeros((8 - MSG, 128), F32)], axis=0) for v in (zero, one)]
        even = jnp.where(lane8 < 64, zero, pltpu.roll(one, 64, 1))
        odd = jnp.where(lane8 < 64, pltpu.roll(zero, 64, 1), one)
        return jnp.concatenate([even, odd], axis=0)

    def camera_sums(read, matrix):
        acc = jnp.zeros((128, 48), F32)
        for group in range(NCHIP // GROUP):
            wide = jnp.concatenate([both_cores(*read(GROUP * group + p)) for p in range(GROUP)], axis=1)
            parts = jnp.concatenate(split3(wide), axis=0).astype(BF16)
            acc = acc + dot_nt(matrix(group), parts)
        return acc[:, 0:16] + acc[:, 16:32] + acc[:, 32:48]

    def column(row):
        wide = jnp.concatenate([row, jnp.zeros((1, 64), F32)], axis=1)
        return jnp.broadcast_to(wide, (128, 128)).T

    for copy in inputs[:4]:
        copy.wait()
    cam_col = column(cam_ref[...].astype(F32))
    fill_col = column(fill_ref[...].astype(F32))
    sub = lax.broadcasted_iota(jnp.int32, (128, 128), 0)
    lane = lax.broadcasted_iota(jnp.int32, (128, 128), 1)
    own_cam = (slab * OWN + sub - 64).astype(F32)
    is_own = (sub >= 64) & (sub < 64 + OWN)
    targets = jnp.where(sub < 64, cam_col, jnp.where(is_own, own_cam, -1.0))

    live = (lane.astype(F32) < fill_col)[:BLK]
    for i in range(18):
        jcm[i] = jnp.where(live, jcm[i], 0.0)

    lane64 = lane[:BLK]
    sub64 = sub[:BLK]

    def spread(values):
        halves = []
        for rest in range(2):
            half = jnp.zeros((BLK, 128), F32)
            for j in range(rest, 9, 2):
                half = jnp.where(lane64 == j // 2, values[j], half)
            halves.append(half)
        return halves

    def message(even, odd):
        return jnp.concatenate([even, odd], axis=0).T[:MSG]

    even, odd = spread(
        [jnp.sum(jcm[j] * jcm[j] + jcm[9 + j] * jcm[9 + j], axis=1, keepdims=True) for j in range(9)]
    )
    odd = jnp.where(lane64 == 4, cam_col[:BLK], odd)
    rhs = rhs_ref[...]
    gap = jnp.zeros((MSG, 64 - OWN), F32)
    none = jnp.zeros((1, OWN), F32)
    rhs_even = jnp.concatenate([rhs[j : j + 1] for j in range(0, 9, 2)], axis=0)
    rhs_odd = jnp.concatenate([rhs[j : j + 1] for j in range(1, 9, 2)] + [none], axis=0)
    first_msg[core, chip] = jnp.concatenate(
        [message(even, odd), jnp.concatenate([rhs_even, gap, rhs_odd, gap], axis=1)], axis=0
    )

    inputs[4].wait()

    def build(k, carry):
        ids = jnp.concatenate([pid_ref[pl.ds(2 * k, 1), :], pid_ref[pl.ds(2 * k + 1, 1), :]], axis=1)
        low = lax.bitwise_and(ids, LO - 1)
        top = lax.shift_right_logical(ids, 6)
        hot = lax.broadcasted_iota(jnp.int32, (HI, CHUNK), 0) == top
        high[k] = jnp.where(hot, 1.0, 0.0).astype(BF16)
        hot_low = jnp.where(lax.broadcasted_iota(jnp.int32, (LO, CHUNK), 0) == low, 1.0, 0.0)
        low_f[k] = hot_low
        low_b[k] = hot_low.astype(BF16)
        return carry

    lax.fori_loop(0, CHUNKS, build, 0)
    inputs[5].wait()
    for i in range(6):
        jpm[i] = jnp.where(live, jpm[i], 0.0)

    pl.semaphore_wait(barrier, len(OFFSETS) + NCAM)
    first_copies = gather_start(first_msg, 0)

    def pair(ref, index, k):
        return jnp.concatenate([ref[index, pl.ds(2 * k, 1), :], ref[index, pl.ds(2 * k + 1, 1), :]], axis=1)

    def scatter(rows_of, count, acc_ref):
        half = NCAM * count * LQ
        acc_ref[...] = jnp.zeros_like(acc_ref)

        def body(step, carry):
            summed = None
            for u in range(STEPS):
                k = step * STEPS + u
                parts = [], []
                for row in rows_of(k):
                    for part, value in zip(parts, split2(row)):
                        part.append(jnp.broadcast_to(value, (LQ, CHUNK)).astype(BF16))
                blocks = [
                    low_b[k, LQ * q : LQ * (q + 1), :] * value
                    for part in parts
                    for q in range(NCAM)
                    for value in part
                ]
                product = dot_nt(jnp.concatenate(blocks, axis=0), high[k])
                summed = product if summed is None else summed + product
            acc_ref[...] += (summed[:half] + summed[half:]).reshape(NCAM, count * LQ, HI)
            return carry

        lax.fori_loop(0, CHUNKS // STEPS, body, 0)

    def jp_products(k):
        a = [pair(jpm, i, k) for i in range(6)]
        return [a[i] * a[j] + a[3 + i] * a[3 + j] for i, j in ((0, 0), (0, 1), (0, 2), (1, 1), (1, 2), (2, 2))]

    scatter(jp_products, 6, v_part)
    v_copies = [
        remote(v_part.at[lax.rem(cam + d, NCAM)], v_recv.at[d - 1], vs.at[d - 1], vr.at[d - 1], cam_peer(d))
        for d in range(1, NCAM)
    ]

    gather_end(first_copies, first_msg, 0)
    lane1 = lax.broadcasted_iota(jnp.int32, (1, 128), 1)

    def same(group):
        blocks = []
        for p in range(GROUP):
            zero, one = [first_msg[c, GROUP * group + p, MSG - 1 : MSG, :] for c in range(2)]
            ids = jnp.where(lane1 < 64, pltpu.roll(zero, 64, 1), one)
            blocks.append(jnp.where(targets == ids, 1.0, 0.0).astype(BF16))
        matrix = jnp.concatenate(blocks, axis=1)
        equal[group] = matrix
        return matrix

    def owned(group):
        place = lax.rem(lane1, 64)
        blocks = []
        for p in range(GROUP):
            source = (GROUP * group + p) * 2 + lax.div(lane1, 64)
            ids = jnp.where(place < OWN, source * OWN + place, -2).astype(F32)
            blocks.append(jnp.where(targets == ids, 1.0, 0.0).astype(BF16))
        return jnp.concatenate(blocks, axis=1)

    lane16 = lax.broadcasted_iota(jnp.int32, (128, 16), 1)
    sub16 = lax.broadcasted_iota(jnp.int32, (128, 16), 0)
    param = (lane16 < 5) | ((lane16 >= 8) & (lane16 < 12))
    mine = param & (sub16 >= 64) & (sub16 < 64 + OWN)

    def read_first(at):
        return lambda other: [first_msg[c, other, MSG * at : MSG * (at + 1), :] for c in range(2)]

    precond = jnp.where(param, camera_sums(read_first(0), same), 0.0) + LAMBDA
    res0 = camera_sums(read_first(1), owned)
    dir0 = res0 / precond

    def apply(it, vec, scalars):
        cols = [jnp.broadcast_to(vec[:BLK, column_of(j) : column_of(j) + 1], (BLK, SLOTS)) for j in range(9)]
        for r in range(2):
            e = jcm[9 * r] * cols[0]
            for j in range(1, 9):
                e = e + jcm[9 * r + j] * cols[j]
            e_ref[r] = e
        for a in range(3):
            t_ref[a] = jpm[a] * e_ref[0] + jpm[3 + a] * e_ref[1]
        scatter(lambda k: [pair(t_ref, a, k) for a in range(3)], 3, q_part.at[it])
        q_copies = [
            remote(
                q_part.at[it, lax.rem(cam + d, NCAM)], q_recv.at[it, d - 1],
                qs.at[it, d - 1], qr.at[it, d - 1], cam_peer(d),
            )
            for d in (2, 1, 3)
        ]
        if it == 0:
            wait_all(v_copies)
            v = v_part[cam] + v_recv[0] + v_recv[1] + v_recv[2]
            v00, v01, v02, v11, v12, v22 = [v[LQ * i : LQ * (i + 1)] for i in range(6)]
            v00, v11, v22 = v00 + MU, v11 + MU, v22 + MU
            c00 = v11 * v22 - v12 * v12
            c01 = v02 * v12 - v01 * v22
            c02 = v01 * v12 - v02 * v11
            c11 = v00 * v22 - v02 * v02
            c12 = v01 * v02 - v00 * v12
            c22 = v00 * v11 - v01 * v01
            det = v00 * c00 + v01 * c01 + v02 * c02
            for i, value in enumerate((c00, c01, c02, c11, c12, c22)):
                cof[i] = value
            cof[6] = det
        wait_all(q_copies)
        q = q_part[it, cam] + q_recv[it, 0] + q_recv[it, 1] + q_recv[it, 2]
        q0, q1, q2 = [q[LQ * i : LQ * (i + 1)] for i in range(3)]
        det = cof[6]
        w0 = (cof[0] * q0 + cof[1] * q1 + cof[2] * q2) / det
        w1 = (cof[1] * q0 + cof[3] * q1 + cof[4] * q2) / det
        w2 = (cof[2] * q0 + cof[4] * q1 + cof[5] * q2) / det
        w_full[it, cam] = jnp.concatenate([w0, w1, w2], axis=0)
        w_copies = [
            remote(w_full.at[it, cam], w_full.at[it, cam], ws.at[it, d - 1], wr.at[it, d - 1], cam_peer(d))
            for d in (2, 1, 3)
        ]
        wait_all(w_copies)
        half = NCAM * 3 * LQ
        for part, value in enumerate(split2(w_full[it].reshape(half, HI))):
            w_split[half * part : half * (part + 1)] = value.astype(BF16)

        def body(step, carry):
            for u in range(STEPS):
                k = step * STEPS + u
                product = dot_nn(w_split[...], high[k])
                product = product[:half] + product[half:]
                for c in range(3):
                    picked = jnp.zeros((LQ, CHUNK), F32)
                    for q in range(NCAM):
                        at = (3 * q + c) * LQ
                        picked = picked + product[at : at + LQ] * low_f[k, LQ * q : LQ * (q + 1), :]
                    row = jnp.sum(picked, axis=0, keepdims=True)
                    w_obs[c, pl.ds(2 * k, 1), :] = row[:, :SLOTS]
                    w_obs[c, pl.ds(2 * k + 1, 1), :] = row[:, SLOTS:]
            return carry

        lax.fori_loop(0, CHUNKS // STEPS, body, 0)
        d = [
            e_ref[r] - (jpm[3 * r] * w_obs[0] + jpm[3 * r + 1] * w_obs[1] + jpm[3 * r + 2] * w_obs[2])
            for r in range(2)
        ]
        even, odd = spread(
            [jnp.sum(jcm[j] * d[0] + jcm[9 + j] * d[1], axis=1, keepdims=True) for j in range(9)]
        )
        if scalars is not None:
            blocks = total(even[:, :8] * vec[:BLK, :8] + odd[:, :8] * vec[:BLK, 8:])
            known = scalars + [LAMBDA * total(jnp.where(mine, vec * vec, 0.0)) + blocks]
            for i, value in enumerate(known):
                odd = jnp.where((lane64 == 4) & (sub64 == i), value, odd)
        buf = msgs.at[it]
        buf[core, chip] = message(even, odd)
        gather_end(gather_start(buf, 1 + it), buf, 1 + it)

    def read_from(it):
        return lambda other: [msgs[it, c, other] for c in range(2)]

    def saved(group):
        return equal[group]

    apply(0, dir0, None)
    image0 = jnp.where(param, camera_sums(read_from(0), saved), 0.0) + LAMBDA * dir0
    rest = res0 - image0
    dir1 = rest / precond
    dots = [total(jnp.where(mine, a * b, 0.0)) for a, b in ((res0, dir0), (dir0, rest), (rest, dir1))]
    apply(1, dir1, dots)

    sc[cam] = jnp.sum(msgs[1, 0] + msgs[1, 1], axis=0)[MSG - 1 : MSG]
    sc_copies = [
        remote(sc.at[cam], sc.at[cam], ss.at[d - 1], sr.at[d - 1], cam_peer(d)) for d in (2, 1, 3)
    ]
    image1 = jnp.where(param, camera_sums(read_from(1), saved), 0.0) + LAMBDA * dir1
    wait_all(sc_copies)
    sums = sc[0] + sc[1] + sc[2] + sc[3]
    aa, bb, cc, dd = [sums[:, 64 + i : 65 + i] for i in range(4)]
    curve = aa - bb
    alpha0 = aa / curve
    keep = -bb / curve
    rz1 = keep * keep * aa + 2.0 * keep * alpha0 * bb + alpha0 * alpha0 * cc
    scale = keep + rz1 / aa
    alpha1 = rz1 / (scale * scale * curve + 2.0 * scale * alpha0 * (bb - cc) + alpha0 * alpha0 * dd)
    dir_last = scale * dir0 + alpha0 * dir1
    img_last = scale * image0 + alpha0 * image1
    sol = alpha0 * dir0 + alpha1 * dir_last
    res = keep * res0 + alpha0 * rest - alpha1 * img_last

    def to_rows(value):
        rows = jnp.concatenate([value, jnp.zeros((128, 112), F32)], axis=1).T[:16]
        rows = jnp.concatenate([rows[column_of(j) : column_of(j) + 1] for j in range(9)], axis=0)
        return rows[:, 64 : 64 + OWN]

    sol_ref[...] = to_rows(sol)
    res_ref[...] = to_rows(res)
    for copy in pending:
        copy.wait_send()


def local(jac_cam, jac_point, point_ids, block_cam, block_fill, rhs):
    dma = pltpu.SemaphoreType.DMA
    vmem = pl.BlockSpec(memory_space=pltpu.VMEM)
    hbm = pl.BlockSpec(memory_space=pltpu.HBM)
    own = jax.ShapeDtypeStruct((9, OWN), F32)
    return pl.pallas_call(
        kernel,
        out_shape=(own, own),
        in_specs=[hbm] * 6,
        out_specs=(vmem, vmem),
        scratch_shapes=[
            pltpu.VMEM((18, BLK, SLOTS), F32),
            pltpu.VMEM((6, BLK, SLOTS), F32),
            pltpu.VMEM((BLK, SLOTS), jnp.int32),
            pltpu.VMEM((1, BLK), jnp.int32),
            pltpu.VMEM((1, BLK), jnp.int32),
            pltpu.VMEM((9, OWN), F32),
            pltpu.VMEM((CHUNKS, LO, CHUNK), BF16),
            pltpu.VMEM((CHUNKS, LO, CHUNK), F32),
            pltpu.VMEM((CHUNKS, HI, CHUNK), BF16),
            pltpu.VMEM((NCHIP // GROUP, 128, GROUP * 128), BF16),
            pltpu.VMEM((3, BLK, SLOTS), F32),
            pltpu.VMEM((3, BLK, SLOTS), F32),
            pltpu.VMEM((2, BLK, SLOTS), F32),
            pltpu.VMEM((NCAM, 6 * LQ, HI), F32),
            pltpu.VMEM((NCAM - 1, 6 * LQ, HI), F32),
            pltpu.VMEM((7, LQ, HI), F32),
            pltpu.VMEM((2, NCAM, 3 * LQ, HI), F32),
            pltpu.VMEM((2, NCAM - 1, 3 * LQ, HI), F32),
            pltpu.VMEM((2, NCAM, 3 * LQ, HI), F32),
            pltpu.VMEM((2 * NCAM * 3 * LQ, HI), BF16),
            pltpu.VMEM((2, NCHIP, 2 * MSG, 128), F32),
            pltpu.VMEM((2, 2, NCHIP, MSG, 128), F32),
            pltpu.VMEM((NCAM, 1, 128), F32),
            dma((6,)),
            dma((3, NCHIP - 1)),
            dma((3, NCHIP - 1)),
            dma((3,)),
            dma((3,)),
            dma((NCAM - 1,)),
            dma((NCAM - 1,)),
            dma((2, NCAM - 1)),
            dma((2, NCAM - 1)),
            dma((2, NCAM - 1)),
            dma((2, NCAM - 1)),
            dma((NCAM - 1,)),
            dma((NCAM - 1,)),
        ],
        compiler_params=pltpu.CompilerParams(
            collective_id=0, has_side_effects=True, vmem_limit_bytes=40 * 1024 * 1024
        ),
        name="schur_cg",
    )(jac_cam, jac_point, point_ids, block_cam.reshape(1, BLK), block_fill.reshape(1, BLK), rhs)


def solution(mesh):
    placed = (
        P(None, ("slab", "cam"), None),
        P(None, ("slab", "cam"), None),
        P(("slab", "cam"), None),
        P(("slab", "cam")),
        P(("slab", "cam")),
        P(None, ("slab", "cam")),
    )
    return jax.shard_map(
        local,
        mesh=mesh,
        in_specs=placed,
        out_specs=(P(None, ("slab", "cam")), P(None, ("slab", "cam"))),
        check_vma=False,
    )
```

```python
import jax
import jax.numpy as jnp
from jax import lax
from jax.experimental import pallas as pl
from jax.experimental.pallas import tpu as pltpu
from jax.sharding import PartitionSpec as P

MU = 1.0
LAMBDA = 0.5

MESH = pl.DeviceIdType.MESH
F32 = jnp.float32
BF16 = jnp.bfloat16

BLK = 64
SLOTS = 128
ITERS = 2
OWN = 48
NX = 4
NZ = 8
NCHIP = NX * NZ
NCAM = 4
HI = 256
LO = 64
LQ = LO // NCAM
CHUNK = 256
CHUNKS = BLK * SLOTS // CHUNK
STEPS_V = 4
STEPS_Q = 16
STEPS_W = 16
MSG = 5
GROUP = 4
GROUPS = NCHIP // (2 * GROUP)

NT = (((1,), (1,)), ((), ()))


def dot_nt(a, b):
    return lax.dot_general(a, b, NT, preferred_element_type=F32)


def dot_nn(a, b):
    return lax.dot_general(a, b, (((1,), (0,)), ((), ())), preferred_element_type=F32)


def split2(v):
    hi = v.astype(BF16).astype(F32)
    return hi, v - hi


def split3(v):
    hi, rest = split2(v)
    mid, low = split2(rest)
    return hi, mid, low


def far_first():
    def hops(offset):
        dx, dz = offset
        return min(dx, NX - dx) + min(dz, NZ - dz)

    offsets = [(dx, dz) for dx in range(NX) for dz in range(NZ) if dx or dz]
    return sorted(offsets, key=hops, reverse=True)


OFFSETS = far_first()


def column_of(j):
    return (j % 2) * 8 + j // 2


def total(v):
    return jnp.sum(jnp.sum(v, axis=0, keepdims=True), axis=1, keepdims=True)


def kernel(
    jc_hbm, jp_hbm, pid_hbm, cam_hbm, fill_hbm, rhs_hbm, sol_ref, res_ref,
    jcm, jpm, pid_ref, cam_ref, fill_ref, rhs_ref, low_b, low_f, high, equal, t_ref, w_obs, e_ref,
    v_part, v_recv, vinv, q_part, q_recv, w_full, w_split, first_msg, msgs, sc,
    precond_ref, vecs, images, dots_ref, ins, cs, cr, ps, pr, vs, vr, qs, qr, ws, wr, ss, sr,
):
    slab = lax.axis_index("slab")
    cam = lax.axis_index("cam")
    core = lax.rem(slab, 2)
    z = lax.rem(lax.div(slab, 2), NZ)
    x = lax.div(slab, 2 * NZ)
    chip = x * NZ + z

    def chip_peer(offset):
        dx, dz = offset
        other = lax.rem(x + dx, NX) * NZ + lax.rem(z + dz, NZ)
        return (other * 2 + core, cam)

    sibling = (chip * 2 + (1 - core), cam)

    def cam_peer(d):
        return (slab, lax.rem(cam + d, NCAM))

    inputs = [
        pltpu.make_async_copy(src, dst, ins.at[i])
        for i, (src, dst) in enumerate(
            (
                (fill_hbm, fill_ref), (cam_hbm, cam_ref), (rhs_hbm, rhs_ref),
                (jc_hbm, jcm), (pid_hbm, pid_ref), (jp_hbm, jpm),
            )
        )
    ]
    for copy in inputs:
        copy.start()
    barrier = pltpu.get_barrier_semaphore()
    for offset in OFFSETS:
        pl.semaphore_signal(barrier, inc=1, device_id=chip_peer(offset), device_id_type=MESH)
    for d in range(1, NCAM):
        pl.semaphore_signal(barrier, inc=1, device_id=cam_peer(d), device_id_type=MESH)
    pl.semaphore_signal(barrier, inc=1, device_id=sibling, device_id_type=MESH)

    def remote(src, dst, send, recv, device):
        copy = pltpu.make_async_remote_copy(
            src_ref=src, dst_ref=dst, send_sem=send, recv_sem=recv, device_id=device, device_id_type=MESH
        )
        copy.start()
        return copy

    def received(ref, send, recv, device):
        return pltpu.make_async_remote_copy(
            src_ref=ref, dst_ref=ref, send_sem=send, recv_sem=recv, device_id=device, device_id_type=MESH
        )

    def wait_all(copies):
        for copy in copies:
            copy.wait_recv()

    def sent(copies):
        for copy in copies:
            copy.wait_send()

    last = NCHIP - 1

    def gather_start(buf, m):
        for i, offset in enumerate(OFFSETS):
            remote(buf.at[core, last], buf.at[core, i], cs.at[m], cr.at[m], chip_peer(offset))

    def gather_middle(buf, m):
        others = buf.at[core, pl.ds(0, last)]
        received(others, cs.at[m], cr.at[m], sibling).wait_recv()
        return remote(buf.at[core], buf.at[core], ps.at[m], pr.at[m], sibling)

    def gather_sent(buf, m):
        others = buf.at[core, pl.ds(0, last)]
        received(others, cs.at[m], cr.at[m], sibling).wait_send()

    lane8 = lax.broadcasted_iota(jnp.int32, (8, 128), 1)

    def side_by_side(first, second):
        first, second = [
            jnp.concatenate([v, jnp.zeros((8 - MSG, 128), F32)], axis=0) for v in (first, second)
        ]
        even = jnp.where(lane8 < 64, first, pltpu.roll(second, 64, 1))
        odd = jnp.where(lane8 < 64, pltpu.roll(first, 64, 1), second)
        return jnp.concatenate([even, odd], axis=0)

    def camera_sums(read, matrix, acc, of_core):
        for group in range(GROUPS):
            slots = range(2 * GROUP * group, 2 * GROUP * (group + 1), 2)
            wide = jnp.concatenate(
                [side_by_side(read(of_core, slot), read(of_core, slot + 1)) for slot in slots], axis=1
            )
            parts = jnp.concatenate(split3(wide), axis=0).astype(BF16)
            acc = acc + dot_nt(matrix(of_core, group), parts)
        return acc

    zero_sums = jnp.zeros((128, 48), F32)

    def three_parts(acc):
        return acc[:, 0:16] + acc[:, 16:32] + acc[:, 32:48]

    def column(row):
        wide = jnp.concatenate([row, jnp.zeros((1, 64), F32)], axis=1)
        return jnp.broadcast_to(wide, (128, 128)).T

    for copy in inputs[:4]:
        copy.wait()
    cam_col = column(cam_ref[...].astype(F32))
    fill_col = column(fill_ref[...].astype(F32))
    sub = lax.broadcasted_iota(jnp.int32, (128, 128), 0)
    lane = lax.broadcasted_iota(jnp.int32, (128, 128), 1)
    own_cam = (slab * OWN + sub - 64).astype(F32)
    is_own = (sub >= 64) & (sub < 64 + OWN)
    targets = jnp.where(sub < 64, cam_col, jnp.where(is_own, own_cam, -1.0))

    live = (lane.astype(F32) < fill_col)[:BLK]
    for i in range(18):
        jcm[i] = jnp.where(live, jcm[i], 0.0)

    lane64 = lane[:BLK]
    sub64 = sub[:BLK]

    def spread(values):
        halves = []
        for rest in range(2):
            half = jnp.zeros((BLK, 128), F32)
            for j in range(rest, 9, 2):
                half = jnp.where(lane64 == j // 2, values[j], half)
            halves.append(half)
        return halves

    def message(even, odd):
        return jnp.concatenate([even, odd], axis=0).T[:MSG]

    even, odd = spread(
        [jnp.sum(jcm[j] * jcm[j] + jcm[9 + j] * jcm[9 + j], axis=1, keepdims=True) for j in range(9)]
    )
    odd = jnp.where(lane64 == 4, cam_col[:BLK], odd)
    rhs = rhs_ref[...]
    gap = jnp.zeros((MSG, 64 - OWN), F32)
    none = jnp.zeros((1, OWN), F32)
    rhs_even = jnp.concatenate([rhs[j : j + 1] for j in range(0, 9, 2)], axis=0)
    rhs_odd = jnp.concatenate([rhs[j : j + 1] for j in range(1, 9, 2)] + [none], axis=0)
    first_msg[core, last] = jnp.concatenate(
        [message(even, odd), jnp.concatenate([rhs_even, gap, rhs_odd, gap], axis=1)], axis=0
    )

    inputs[4].wait()

    def build(k, carry):
        ids = jnp.concatenate([pid_ref[pl.ds(2 * k, 1), :], pid_ref[pl.ds(2 * k + 1, 1), :]], axis=1)
        low = lax.bitwise_and(ids, LO - 1)
        top = lax.shift_right_logical(ids, 6)
        hot = lax.broadcasted_iota(jnp.int32, (HI, CHUNK), 0) == top
        high[k] = jnp.where(hot, 1.0, 0.0).astype(BF16)
        hot_low = jnp.where(lax.broadcasted_iota(jnp.int32, (LO, CHUNK), 0) == low, 1.0, 0.0)
        low_f[k] = hot_low
        low_b[k] = hot_low.astype(BF16)
        return carry

    lax.fori_loop(0, CHUNKS, build, 0)
    inputs[5].wait()
    for i in range(6):
        jpm[i] = jnp.where(live, jpm[i], 0.0)

    pl.semaphore_wait(barrier, len(OFFSETS) + NCAM)
    gather_start(first_msg, 0)

    def pair(ref, index, k):
        return jnp.concatenate([ref[index, pl.ds(2 * k, 1), :], ref[index, pl.ds(2 * k + 1, 1), :]], axis=1)

    def scatter(rows_of, count, acc_ref, steps):
        half = NCAM * count * LQ
        acc_ref[...] = jnp.zeros_like(acc_ref)

        def body(step, carry):
            summed = None
            for u in range(steps):
                k = step * steps + u
                parts = [], []
                for row in rows_of(k):
                    for part, value in zip(parts, split2(row)):
                        part.append(jnp.broadcast_to(value, (LQ, CHUNK)).astype(BF16))
                blocks = [
                    low_b[k, LQ * q : LQ * (q + 1), :] * value
                    for part in parts
                    for q in range(NCAM)
                    for value in part
                ]
                product = dot_nt(jnp.concatenate(blocks, axis=0), high[k])
                summed = product if summed is None else summed + product
            acc_ref[...] += (summed[:half] + summed[half:]).reshape(NCAM, count * LQ, HI)
            return carry

        lax.fori_loop(0, CHUNKS // steps, body, 0)

    def jp_products(k):
        a = [pair(jpm, i, k) for i in range(6)]
        return [a[i] * a[j] + a[3 + i] * a[3 + j] for i, j in ((0, 0), (0, 1), (0, 2), (1, 1), (1, 2), (2, 2))]

    scatter(jp_products, 6, v_part, STEPS_V)
    first_swap = gather_middle(first_msg, 0)
    v_copies = [
        remote(v_part.at[lax.rem(cam + d, NCAM)], v_recv.at[d - 1], vs.at[d - 1], vr.at[d - 1], cam_peer(d))
        for d in range(1, NCAM)
    ]

    lane1 = lax.broadcasted_iota(jnp.int32, (1, 128), 1)

    def same(of_core, group):
        blocks = []
        for p in range(GROUP):
            slot = 2 * (GROUP * group + p)
            first, second = [first_msg[of_core, slot + i, MSG - 1 : MSG, :] for i in range(2)]
            ids = jnp.where(lane1 < 64, pltpu.roll(first, 64, 1), second)
            blocks.append(jnp.where(targets == ids, 1.0, 0.0).astype(BF16))
        matrix = jnp.concatenate(blocks, axis=1)
        equal[of_core, group] = matrix
        return matrix

    def owned(of_core, group):
        place = lax.rem(lane1, 64)
        blocks = []
        for p in range(GROUP):
            slot = 2 * (GROUP * group + p)
            first, second = [
                lax.rem(x - dx + NX, NX) * NZ + lax.rem(z - dz + NZ, NZ)
                for dx, dz in (OFFSETS + [(0, 0)])[slot : slot + 2]
            ]
            source = jnp.where(lane1 < 64, first, second) * 2 + of_core
            ids = jnp.where(place < OWN, source * OWN + place, -2).astype(F32)
            blocks.append(jnp.where(targets == ids, 1.0, 0.0).astype(BF16))
        return jnp.concatenate(blocks, axis=1)

    def saved(of_core, group):
        return equal[of_core, group]

    lane16 = lax.broadcasted_iota(jnp.int32, (128, 16), 1)
    sub16 = lax.broadcasted_iota(jnp.int32, (128, 16), 0)
    param = (lane16 < 5) | ((lane16 >= 8) & (lane16 < 12))
    mine = param & (sub16 >= 64) & (sub16 < 64 + OWN)

    def read_first(at):
        return lambda of_core, slot: first_msg[of_core, slot, MSG * at : MSG * (at + 1), :]

    diag_sums = camera_sums(read_first(0), same, zero_sums, core)
    rhs_sums = camera_sums(read_first(1), owned, zero_sums, core)
    first_swap.wait_recv()
    diag_sums = camera_sums(read_first(0), same, diag_sums, 1 - core)
    rhs_sums = camera_sums(read_first(1), owned, rhs_sums, 1 - core)
    precond = jnp.where(param, three_parts(diag_sums), 0.0) + LAMBDA
    res0 = three_parts(rhs_sums)
    precond_ref[...] = precond
    vecs[0] = res0 / precond
    vecs[1] = res0
    dots_ref[...] = jnp.zeros((1, 128), F32)

    def apply(it, carry):
        vec = vecs[it]
        cols = [jnp.broadcast_to(vec[:BLK, column_of(j) : column_of(j) + 1], (BLK, SLOTS)) for j in range(9)]
        for r in range(2):
            e = jcm[9 * r] * cols[0]
            for j in range(1, 9):
                e = e + jcm[9 * r + j] * cols[j]
            e_ref[r] = e
        for a in range(3):
            t_ref[a] = jpm[a] * e_ref[0] + jpm[3 + a] * e_ref[1]
        scatter(lambda k: [pair(t_ref, a, k) for a in range(3)], 3, q_part.at[it], STEPS_Q)
        q_copies = [
            remote(
                q_part.at[it, lax.rem(cam + d, NCAM)], q_recv.at[it, d - 1],
                qs.at[it, d - 1], qr.at[it, d - 1], cam_peer(d),
            )
            for d in (2, 1, 3)
        ]
        square = LAMBDA * total(jnp.where(mine, vec * vec, 0.0))
        square = square + total(e_ref[0] * e_ref[0] + e_ref[1] * e_ref[1])

        @pl.when(it == 0)
        def invert():
            wait_all(v_copies)
            v = v_part[cam] + v_recv[0] + v_recv[1] + v_recv[2]
            v00, v01, v02, v11, v12, v22 = [v[LQ * i : LQ * (i + 1)] for i in range(6)]
            v00, v11, v22 = v00 + MU, v11 + MU, v22 + MU
            c00 = v11 * v22 - v12 * v12
            c01 = v02 * v12 - v01 * v22
            c02 = v01 * v12 - v02 * v11
            c11 = v00 * v22 - v02 * v02
            c12 = v01 * v02 - v00 * v12
            c22 = v00 * v11 - v01 * v01
            det = v00 * c00 + v01 * c01 + v02 * c02
            for i, value in enumerate((c00, c01, c02, c11, c12, c22)):
                vinv[i] = value / det

        wait_all(q_copies)
        q = q_part[it, cam] + q_recv[it, 0] + q_recv[it, 1] + q_recv[it, 2]
        q0, q1, q2 = [q[LQ * i : LQ * (i + 1)] for i in range(3)]
        w0 = vinv[0] * q0 + vinv[1] * q1 + vinv[2] * q2
        w1 = vinv[1] * q0 + vinv[3] * q1 + vinv[4] * q2
        w2 = vinv[2] * q0 + vinv[4] * q1 + vinv[5] * q2
        w_full[it, cam] = jnp.concatenate([w0, w1, w2], axis=0)
        w_copies = [
            remote(w_full.at[it, cam], w_full.at[it, cam], ws.at[it, d - 1], wr.at[it, d - 1], cam_peer(d))
            for d in (2, 1, 3)
        ]
        square = square - total(q0 * w0 + q1 * w1 + q2 * w2)
        sc[it, cam] = jnp.where(lane1 == 3, square, dots_ref[...])
        sc_copies = [
            remote(sc.at[it, cam], sc.at[it, cam], ss.at[it, d - 1], sr.at[it, d - 1], cam_peer(d))
            for d in (2, 1, 3)
        ]
        wait_all(w_copies)
        half = NCAM * 3 * LQ
        for part, value in enumerate(split2(w_full[it].reshape(half, HI))):
            w_split[half * part : half * (part + 1)] = value.astype(BF16)

        def body(step, carry):
            for u in range(STEPS_W):
                k = step * STEPS_W + u
                product = dot_nn(w_split[...], high[k])
                product = product[:half] + product[half:]
                for c in range(3):
                    picked = jnp.zeros((LQ, CHUNK), F32)
                    for q in range(NCAM):
                        at = (3 * q + c) * LQ
                        picked = picked + product[at : at + LQ] * low_f[k, LQ * q : LQ * (q + 1), :]
                    row = jnp.sum(picked, axis=0, keepdims=True)
                    w_obs[c, pl.ds(2 * k, 1), :] = row[:, :SLOTS]
                    w_obs[c, pl.ds(2 * k + 1, 1), :] = row[:, SLOTS:]
            return carry

        lax.fori_loop(0, CHUNKS // STEPS_W, body, 0)
        d = [
            e_ref[r] - (jpm[3 * r] * w_obs[0] + jpm[3 * r + 1] * w_obs[1] + jpm[3 * r + 2] * w_obs[2])
            for r in range(2)
        ]
        even, odd = spread(
            [jnp.sum(jcm[j] * d[0] + jcm[9 + j] * d[1], axis=1, keepdims=True) for j in range(9)]
        )
        wait_all(sc_copies)
        sums = column((sc[it, 0] + sc[it, 1] + sc[it, 2] + sc[it, 3])[:, :64])[:BLK]
        odd = jnp.where((lane64 == 4) & (sub64 < 4), sums, odd)
        buf = msgs.at[it]
        buf[core, last] = message(even, odd)
        gather_start(buf, 1 + it)
        sent(q_copies + w_copies + sc_copies)
        swap = gather_middle(buf, 1 + it)

        def read(of_core, slot):
            return msgs[it, of_core, slot]

        acc = camera_sums(read, saved, zero_sums, core)
        swap.wait_recv()
        acc = camera_sums(read, saved, acc, 1 - core)
        image = jnp.where(param, three_parts(acc), 0.0) + LAMBDA * vec
        images[it] = image

        @pl.when(it == 0)
        def prepare():
            res0 = vecs[1]
            rest = res0 - image
            following = rest / precond_ref[...]
            row = jnp.zeros((1, 128), F32)
            for i, (a, b) in enumerate(((res0, vec), (vec, rest), (rest, following))):
                row = jnp.where(lane1 == i, total(jnp.where(mine, a * b, 0.0)), row)
            dots_ref[...] = row
            vecs[1] = following
            vecs[2] = res0

        swap.wait_send()
        gather_sent(buf, 1 + it)
        return carry

    lax.fori_loop(0, ITERS, apply, 0)
    dir0, dir1, res0 = vecs[0], vecs[1], vecs[2]
    image0, image1 = images[0], images[1]
    rest = res0 - image0
    sums = jnp.sum(msgs[1, 0] + msgs[1, 1], axis=0)[MSG - 1 : MSG]
    aa, bb, cc, dd = [sums[:, 64 + i : 65 + i] for i in range(4)]
    curve = aa - bb
    alpha0 = aa / curve
    keep = -bb / curve
    rz1 = keep * keep * aa + 2.0 * keep * alpha0 * bb + alpha0 * alpha0 * cc
    scale = keep + rz1 / aa
    alpha1 = rz1 / (scale * scale * curve + 2.0 * scale * alpha0 * (bb - cc) + alpha0 * alpha0 * dd)
    dir_last = scale * dir0 + alpha0 * dir1
    img_last = scale * image0 + alpha0 * image1
    sol = alpha0 * dir0 + alpha1 * dir_last
    res = keep * res0 + alpha0 * rest - alpha1 * img_last

    def to_rows(value):
        rows = jnp.concatenate([value, jnp.zeros((128, 112), F32)], axis=1).T[:16]
        rows = jnp.concatenate([rows[column_of(j) : column_of(j) + 1] for j in range(9)], axis=0)
        return rows[:, 64 : 64 + OWN]

    sol_ref[...] = to_rows(sol)
    res_ref[...] = to_rows(res)
    sent(v_copies + [first_swap])
    gather_sent(first_msg, 0)


def local(jac_cam, jac_point, point_ids, block_cam, block_fill, rhs):
    dma = pltpu.SemaphoreType.DMA
    vmem = pl.BlockSpec(memory_space=pltpu.VMEM)
    hbm = pl.BlockSpec(memory_space=pltpu.HBM)
    own = jax.ShapeDtypeStruct((9, OWN), F32)
    return pl.pallas_call(
        kernel,
        out_shape=(own, own),
        in_specs=[hbm] * 6,
        out_specs=(vmem, vmem),
        scratch_shapes=[
            pltpu.VMEM((18, BLK, SLOTS), F32),
            pltpu.VMEM((6, BLK, SLOTS), F32),
            pltpu.VMEM((BLK, SLOTS), jnp.int32),
            pltpu.VMEM((1, BLK), jnp.int32),
            pltpu.VMEM((1, BLK), jnp.int32),
            pltpu.VMEM((9, OWN), F32),
            pltpu.VMEM((CHUNKS, LO, CHUNK), BF16),
            pltpu.VMEM((CHUNKS, LO, CHUNK), F32),
            pltpu.VMEM((CHUNKS, HI, CHUNK), BF16),
            pltpu.VMEM((2, GROUPS, 128, GROUP * 128), BF16),
            pltpu.VMEM((3, BLK, SLOTS), F32),
            pltpu.VMEM((3, BLK, SLOTS), F32),
            pltpu.VMEM((2, BLK, SLOTS), F32),
            pltpu.VMEM((NCAM, 6 * LQ, HI), F32),
            pltpu.VMEM((NCAM - 1, 6 * LQ, HI), F32),
            pltpu.VMEM((6, LQ, HI), F32),
            pltpu.VMEM((2, NCAM, 3 * LQ, HI), F32),
            pltpu.VMEM((2, NCAM - 1, 3 * LQ, HI), F32),
            pltpu.VMEM((2, NCAM, 3 * LQ, HI), F32),
            pltpu.VMEM((2 * NCAM * 3 * LQ, HI), BF16),
            pltpu.VMEM((2, NCHIP, 2 * MSG, 128), F32),
            pltpu.VMEM((2, 2, NCHIP, MSG, 128), F32),
            pltpu.VMEM((2, NCAM, 1, 128), F32),
            pltpu.VMEM((128, 16), F32),
            pltpu.VMEM((3, 128, 16), F32),
            pltpu.VMEM((2, 128, 16), F32),
            pltpu.VMEM((1, 128), F32),
            dma((6,)),
            dma((3,)),
            dma((3,)),
            dma((3,)),
            dma((3,)),
            dma((NCAM - 1,)),
            dma((NCAM - 1,)),
            dma((2, NCAM - 1)),
            dma((2, NCAM - 1)),
            dma((2, NCAM - 1)),
            dma((2, NCAM - 1)),
            dma((2, NCAM - 1)),
            dma((2, NCAM - 1)),
        ],
        compiler_params=pltpu.CompilerParams(
            collective_id=0, has_side_effects=True, vmem_limit_bytes=60 * 1024 * 1024
        ),
        name="schur_cg",
    )(jac_cam, jac_point, point_ids, block_cam.reshape(1, BLK), block_fill.reshape(1, BLK), rhs)


def solution(mesh):
    placed = (
        P(None, ("slab", "cam"), None),
        P(None, ("slab", "cam"), None),
        P(("slab", "cam"), None),
        P(("slab", "cam")),
        P(("slab", "cam")),
        P(None, ("slab", "cam")),
    )
    return jax.shard_map(
        local,
        mesh=mesh,
        in_specs=placed,
        out_specs=(P(None, ("slab", "cam")), P(None, ("slab", "cam"))),
        check_vma=False,
    )
```

```python
import jax
import jax.numpy as jnp
from jax import lax
from jax.experimental import pallas as pl
from jax.experimental.pallas import tpu as pltpu
from jax.sharding import PartitionSpec as P

MU = 1.0
LAMBDA = 0.5

MESH = pl.DeviceIdType.MESH
F32 = jnp.float32
BF16 = jnp.bfloat16

BLK = 64
SLOTS = 128
ITERS = 2
OWN = 48
NX = 4
NZ = 8
NCHIP = NX * NZ
NCAM = 4
HI = 256
LO = 64
LQ = LO // NCAM
CHUNK = 256
CHUNKS = BLK * SLOTS // CHUNK
STEPS_V = 4
STEPS_Q = 32
STEPS_W = 16
MSG = 5
GROUP = 4
GROUPS = NCHIP // (2 * GROUP)

NT = (((1,), (1,)), ((), ()))


def dot_nt(a, b):
    return lax.dot_general(a, b, NT, preferred_element_type=F32)


def dot_nn(a, b):
    return lax.dot_general(a, b, (((1,), (0,)), ((), ())), preferred_element_type=F32)


def split2(v):
    hi = v.astype(BF16).astype(F32)
    return hi, v - hi


def split3(v):
    hi, rest = split2(v)
    mid, low = split2(rest)
    return hi, mid, low


def far_first():
    def hops(offset):
        dx, dz = offset
        return min(dx, NX - dx) + min(dz, NZ - dz)

    offsets = [(dx, dz) for dx in range(NX) for dz in range(NZ) if dx or dz]
    return sorted(offsets, key=hops, reverse=True)


OFFSETS = far_first()


def column_of(j):
    return (j % 2) * 8 + j // 2


def total(v):
    return jnp.sum(jnp.sum(v, axis=0, keepdims=True), axis=1, keepdims=True)


def kernel(
    jc_hbm, jp_hbm, pid_hbm, cam_hbm, fill_hbm, rhs_hbm, sol_ref, res_ref,
    jcm, jpm, pid_ref, cam_ref, fill_ref, rhs_ref, low_b, low_f, high, equal, t_ref, w_obs, e_ref,
    v_part, v_recv, vinv, q_part, q_recv, w_full, w_split, first_msg, msgs, sc,
    precond_ref, vecs, images, dots_ref, ins, cs, cr, ps, pr, vs, vr, qs, qr, ws, wr, ss, sr,
):
    slab = lax.axis_index("slab")
    cam = lax.axis_index("cam")
    core = lax.rem(slab, 2)
    z = lax.rem(lax.div(slab, 2), NZ)
    x = lax.div(slab, 2 * NZ)
    chip = x * NZ + z

    def chip_peer(offset):
        dx, dz = offset
        other = lax.rem(x + dx, NX) * NZ + lax.rem(z + dz, NZ)
        return (other * 2 + core, cam)

    sibling = (chip * 2 + (1 - core), cam)

    def cam_peer(d):
        return (slab, lax.rem(cam + d, NCAM))

    barrier = pltpu.get_barrier_semaphore()
    for offset in OFFSETS:
        pl.semaphore_signal(barrier, inc=1, device_id=chip_peer(offset), device_id_type=MESH)
    for d in range(1, NCAM):
        pl.semaphore_signal(barrier, inc=1, device_id=cam_peer(d), device_id_type=MESH)
    pl.semaphore_signal(barrier, inc=1, device_id=sibling, device_id_type=MESH)

    inputs = [
        pltpu.make_async_copy(src, dst, ins.at[i])
        for i, (src, dst) in enumerate(
            (
                (fill_hbm, fill_ref), (cam_hbm, cam_ref), (rhs_hbm, rhs_ref),
                (jc_hbm, jcm), (pid_hbm, pid_ref), (jp_hbm, jpm),
            )
        )
    ]
    for copy in inputs:
        copy.start()
    def remote(src, dst, send, recv, device):
        copy = pltpu.make_async_remote_copy(
            src_ref=src, dst_ref=dst, send_sem=send, recv_sem=recv, device_id=device, device_id_type=MESH
        )
        copy.start()
        return copy

    def received(ref, send, recv, device):
        return pltpu.make_async_remote_copy(
            src_ref=ref, dst_ref=ref, send_sem=send, recv_sem=recv, device_id=device, device_id_type=MESH
        )

    def wait_all(copies):
        for copy in copies:
            copy.wait_recv()

    def sent(copies):
        for copy in copies:
            copy.wait_send()

    last = NCHIP - 1

    def gather_start(buf, m):
        for i, offset in enumerate(OFFSETS):
            remote(buf.at[core, last], buf.at[core, i], cs.at[m], cr.at[m], chip_peer(offset))

    def gather_middle(buf, m):
        others = buf.at[core, pl.ds(0, last)]
        received(others, cs.at[m], cr.at[m], sibling).wait_recv()
        return remote(buf.at[core], buf.at[core], ps.at[m], pr.at[m], sibling)

    def gather_sent(buf, m):
        others = buf.at[core, pl.ds(0, last)]
        received(others, cs.at[m], cr.at[m], sibling).wait_send()

    lane8 = lax.broadcasted_iota(jnp.int32, (8, 128), 1)

    def side_by_side(first, second):
        first, second = [
            jnp.concatenate([v, jnp.zeros((8 - MSG, 128), F32)], axis=0) for v in (first, second)
        ]
        even = jnp.where(lane8 < 64, first, pltpu.roll(second, 64, 1))
        odd = jnp.where(lane8 < 64, pltpu.roll(first, 64, 1), second)
        return jnp.concatenate([even, odd], axis=0)

    def camera_sums(read, matrix, acc, of_core):
        for group in range(GROUPS):
            slots = range(2 * GROUP * group, 2 * GROUP * (group + 1), 2)
            wide = jnp.concatenate(
                [side_by_side(read(of_core, slot), read(of_core, slot + 1)) for slot in slots], axis=1
            )
            parts = jnp.concatenate(split3(wide), axis=0).astype(BF16)
            acc = acc + dot_nt(matrix(of_core, group), parts)
        return acc

    zero_sums = jnp.zeros((128, 48), F32)

    def three_parts(acc):
        return acc[:, 0:16] + acc[:, 16:32] + acc[:, 32:48]

    def column(row):
        wide = jnp.concatenate([row, jnp.zeros((1, 64), F32)], axis=1)
        return jnp.broadcast_to(wide, (128, 128)).T

    for copy in inputs[:4]:
        copy.wait()
    cam_col = column(cam_ref[...].astype(F32))
    fill_col = column(fill_ref[...].astype(F32))
    sub = lax.broadcasted_iota(jnp.int32, (128, 128), 0)
    lane = lax.broadcasted_iota(jnp.int32, (128, 128), 1)
    own_cam = (slab * OWN + sub - 64).astype(F32)
    is_own = (sub >= 64) & (sub < 64 + OWN)
    targets = jnp.where(sub < 64, cam_col, jnp.where(is_own, own_cam, -1.0))

    live = (lane.astype(F32) < fill_col)[:BLK]
    for i in range(18):
        jcm[i] = jnp.where(live, jcm[i], 0.0)

    lane64 = lane[:BLK]
    sub64 = sub[:BLK]

    def spread(values):
        halves = []
        for rest in range(2):
            half = jnp.zeros((BLK, 128), F32)
            for j in range(rest, 9, 2):
                half = jnp.where(lane64 == j // 2, values[j], half)
            halves.append(half)
        return halves

    def message(even, odd):
        return jnp.concatenate([even, odd], axis=0).T[:MSG]

    even, odd = spread(
        [jnp.sum(jcm[j] * jcm[j] + jcm[9 + j] * jcm[9 + j], axis=1, keepdims=True) for j in range(9)]
    )
    odd = jnp.where(lane64 == 4, cam_col[:BLK], odd)
    rhs = rhs_ref[...]
    gap = jnp.zeros((MSG, 64 - OWN), F32)
    none = jnp.zeros((1, OWN), F32)
    rhs_even = jnp.concatenate([rhs[j : j + 1] for j in range(0, 9, 2)], axis=0)
    rhs_odd = jnp.concatenate([rhs[j : j + 1] for j in range(1, 9, 2)] + [none], axis=0)
    first_msg[core, last] = jnp.concatenate(
        [message(even, odd), jnp.concatenate([rhs_even, gap, rhs_odd, gap], axis=1)], axis=0
    )

    inputs[4].wait()

    def build(k, carry):
        ids = jnp.concatenate([pid_ref[pl.ds(2 * k, 1), :], pid_ref[pl.ds(2 * k + 1, 1), :]], axis=1)
        low = lax.bitwise_and(ids, LO - 1)
        top = lax.shift_right_logical(ids, 6)
        hot = lax.broadcasted_iota(jnp.int32, (HI, CHUNK), 0) == top
        high[k] = jnp.where(hot, 1.0, 0.0).astype(BF16)
        hot_low = jnp.where(lax.broadcasted_iota(jnp.int32, (LO, CHUNK), 0) == low, 1.0, 0.0)
        low_f[k] = hot_low
        low_b[k] = hot_low.astype(BF16)
        return carry

    lax.fori_loop(0, CHUNKS, build, 0)
    inputs[5].wait()
    for i in range(6):
        jpm[i] = jnp.where(live, jpm[i], 0.0)

    pl.semaphore_wait(barrier, len(OFFSETS) + NCAM)
    gather_start(first_msg, 0)

    def pair(ref, index, k):
        return jnp.concatenate([ref[index, pl.ds(2 * k, 1), :], ref[index, pl.ds(2 * k + 1, 1), :]], axis=1)

    def scatter(rows_of, count, acc_ref, steps):
        half = NCAM * count * LQ
        acc_ref[...] = jnp.zeros_like(acc_ref)

        def body(step, carry):
            summed = None
            for u in range(steps):
                k = step * steps + u
                parts = [], []
                for row in rows_of(k):
                    for part, value in zip(parts, split2(row)):
                        part.append(jnp.broadcast_to(value, (LQ, CHUNK)).astype(BF16))
                blocks = [
                    low_b[k, LQ * q : LQ * (q + 1), :] * value
                    for part in parts
                    for q in range(NCAM)
                    for value in part
                ]
                product = dot_nt(jnp.concatenate(blocks, axis=0), high[k])
                summed = product if summed is None else summed + product
            acc_ref[...] += (summed[:half] + summed[half:]).reshape(NCAM, count * LQ, HI)
            return carry

        lax.fori_loop(0, CHUNKS // steps, body, 0)

    def jp_products(k):
        a = [pair(jpm, i, k) for i in range(6)]
        return [a[i] * a[j] + a[3 + i] * a[3 + j] for i, j in ((0, 0), (0, 1), (0, 2), (1, 1), (1, 2), (2, 2))]

    scatter(jp_products, 6, v_part, STEPS_V)
    first_swap = gather_middle(first_msg, 0)
    v_copies = [
        remote(v_part.at[lax.rem(cam + d, NCAM)], v_recv.at[d - 1], vs.at[d - 1], vr.at[d - 1], cam_peer(d))
        for d in range(1, NCAM)
    ]

    lane1 = lax.broadcasted_iota(jnp.int32, (1, 128), 1)

    def same(of_core, group):
        blocks = []
        for p in range(GROUP):
            slot = 2 * (GROUP * group + p)
            first, second = [first_msg[of_core, slot + i, MSG - 1 : MSG, :] for i in range(2)]
            ids = jnp.where(lane1 < 64, pltpu.roll(first, 64, 1), second)
            blocks.append(jnp.where(targets == ids, 1.0, 0.0).astype(BF16))
        matrix = jnp.concatenate(blocks, axis=1)
        equal[of_core, group] = matrix
        return matrix

    def owned(of_core, group):
        place = lax.rem(lane1, 64)
        blocks = []
        for p in range(GROUP):
            slot = 2 * (GROUP * group + p)
            first, second = [
                lax.rem(x - dx + NX, NX) * NZ + lax.rem(z - dz + NZ, NZ)
                for dx, dz in (OFFSETS + [(0, 0)])[slot : slot + 2]
            ]
            source = jnp.where(lane1 < 64, first, second) * 2 + of_core
            ids = jnp.where(place < OWN, source * OWN + place, -2).astype(F32)
            blocks.append(jnp.where(targets == ids, 1.0, 0.0).astype(BF16))
        return jnp.concatenate(blocks, axis=1)

    def saved(of_core, group):
        return equal[of_core, group]

    lane16 = lax.broadcasted_iota(jnp.int32, (128, 16), 1)
    sub16 = lax.broadcasted_iota(jnp.int32, (128, 16), 0)
    param = (lane16 < 5) | ((lane16 >= 8) & (lane16 < 12))
    mine = param & (sub16 >= 64) & (sub16 < 64 + OWN)

    def read_first(at):
        return lambda of_core, slot: first_msg[of_core, slot, MSG * at : MSG * (at + 1), :]

    diag_sums = camera_sums(read_first(0), same, zero_sums, core)
    rhs_sums = camera_sums(read_first(1), owned, zero_sums, core)
    first_swap.wait_recv()
    diag_sums = camera_sums(read_first(0), same, diag_sums, 1 - core)
    rhs_sums = camera_sums(read_first(1), owned, rhs_sums, 1 - core)
    precond = jnp.where(param, three_parts(diag_sums), 0.0) + LAMBDA
    res0 = three_parts(rhs_sums)
    precond_ref[...] = precond
    vecs[0] = res0 / precond
    vecs[1] = res0
    dots_ref[...] = jnp.zeros((1, 128), F32)

    def apply(it, carry):
        vec = vecs[it]
        cols = [jnp.broadcast_to(vec[:BLK, column_of(j) : column_of(j) + 1], (BLK, SLOTS)) for j in range(9)]
        for r in range(2):
            e = jcm[9 * r] * cols[0]
            for j in range(1, 9):
                e = e + jcm[9 * r + j] * cols[j]
            e_ref[r] = e
        for a in range(3):
            t_ref[a] = jpm[a] * e_ref[0] + jpm[3 + a] * e_ref[1]
        scatter(lambda k: [pair(t_ref, a, k) for a in range(3)], 3, q_part.at[it], STEPS_Q)
        q_copies = [
            remote(
                q_part.at[it, lax.rem(cam + d, NCAM)], q_recv.at[it, d - 1],
                qs.at[it, d - 1], qr.at[it, d - 1], cam_peer(d),
            )
            for d in (2, 1, 3)
        ]
        square = LAMBDA * total(jnp.where(mine, vec * vec, 0.0))
        square = square + total(e_ref[0] * e_ref[0] + e_ref[1] * e_ref[1])

        @pl.when(it == 0)
        def invert():
            wait_all(v_copies)
            v = v_part[cam] + v_recv[0] + v_recv[1] + v_recv[2]
            v00, v01, v02, v11, v12, v22 = [v[LQ * i : LQ * (i + 1)] for i in range(6)]
            v00, v11, v22 = v00 + MU, v11 + MU, v22 + MU
            c00 = v11 * v22 - v12 * v12
            c01 = v02 * v12 - v01 * v22
            c02 = v01 * v12 - v02 * v11
            c11 = v00 * v22 - v02 * v02
            c12 = v01 * v02 - v00 * v12
            c22 = v00 * v11 - v01 * v01
            det = v00 * c00 + v01 * c01 + v02 * c02
            for i, value in enumerate((c00, c01, c02, c11, c12, c22)):
                vinv[i] = value / det

        wait_all(q_copies)
        q = q_part[it, cam] + q_recv[it, 0] + q_recv[it, 1] + q_recv[it, 2]
        q0, q1, q2 = [q[LQ * i : LQ * (i + 1)] for i in range(3)]
        w0 = vinv[0] * q0 + vinv[1] * q1 + vinv[2] * q2
        w1 = vinv[1] * q0 + vinv[3] * q1 + vinv[4] * q2
        w2 = vinv[2] * q0 + vinv[4] * q1 + vinv[5] * q2
        w_full[it, cam] = jnp.concatenate([w0, w1, w2], axis=0)
        w_copies = [
            remote(w_full.at[it, cam], w_full.at[it, cam], ws.at[it, d - 1], wr.at[it, d - 1], cam_peer(d))
            for d in (2, 1, 3)
        ]
        square = square - total(q0 * w0 + q1 * w1 + q2 * w2)
        sc[it, cam] = jnp.where(lane1 == 3, square, dots_ref[...])
        sc_copies = [
            remote(sc.at[it, cam], sc.at[it, cam], ss.at[it, d - 1], sr.at[it, d - 1], cam_peer(d))
            for d in (2, 1, 3)
        ]
        wait_all(w_copies)
        half = NCAM * 3 * LQ
        for part, value in enumerate(split2(w_full[it].reshape(half, HI))):
            w_split[half * part : half * (part + 1)] = value.astype(BF16)

        def body(step, carry):
            for u in range(STEPS_W):
                k = step * STEPS_W + u
                product = dot_nn(w_split[...], high[k])
                product = product[:half] + product[half:]
                for c in range(3):
                    picked = jnp.zeros((LQ, CHUNK), F32)
                    for q in range(NCAM):
                        at = (3 * q + c) * LQ
                        picked = picked + product[at : at + LQ] * low_f[k, LQ * q : LQ * (q + 1), :]
                    row = jnp.sum(picked, axis=0, keepdims=True)
                    w_obs[c, pl.ds(2 * k, 1), :] = row[:, :SLOTS]
                    w_obs[c, pl.ds(2 * k + 1, 1), :] = row[:, SLOTS:]
            return carry

        lax.fori_loop(0, CHUNKS // STEPS_W, body, 0)
        d = [
            e_ref[r] - (jpm[3 * r] * w_obs[0] + jpm[3 * r + 1] * w_obs[1] + jpm[3 * r + 2] * w_obs[2])
            for r in range(2)
        ]
        even, odd = spread(
            [jnp.sum(jcm[j] * d[0] + jcm[9 + j] * d[1], axis=1, keepdims=True) for j in range(9)]
        )
        wait_all(sc_copies)
        sums = column((sc[it, 0] + sc[it, 1] + sc[it, 2] + sc[it, 3])[:, :64])[:BLK]
        odd = jnp.where((lane64 == 4) & (sub64 < 4), sums, odd)
        buf = msgs.at[it]
        buf[core, last] = message(even, odd)
        gather_start(buf, 1 + it)
        sent(q_copies + w_copies + sc_copies)
        swap = gather_middle(buf, 1 + it)

        def read(of_core, slot):
            return msgs[it, of_core, slot]

        acc = camera_sums(read, saved, zero_sums, core)
        swap.wait_recv()
        acc = camera_sums(read, saved, acc, 1 - core)
        image = jnp.where(param, three_parts(acc), 0.0) + LAMBDA * vec
        images[it] = image

        @pl.when(it == 0)
        def prepare():
            res0 = vecs[1]
            rest = res0 - image
            following = rest / precond_ref[...]
            row = jnp.zeros((1, 128), F32)
            for i, (a, b) in enumerate(((res0, vec), (vec, rest), (rest, following))):
                row = jnp.where(lane1 == i, total(jnp.where(mine, a * b, 0.0)), row)
            dots_ref[...] = row
            vecs[1] = following
            vecs[2] = res0

        swap.wait_send()
        gather_sent(buf, 1 + it)
        return carry

    lax.fori_loop(0, ITERS, apply, 0)
    dir0, dir1, res0 = vecs[0], vecs[1], vecs[2]
    image0, image1 = images[0], images[1]
    rest = res0 - image0
    sums = jnp.sum(msgs[1, 0] + msgs[1, 1], axis=0)[MSG - 1 : MSG]
    aa, bb, cc, dd = [sums[:, 64 + i : 65 + i] for i in range(4)]
    curve = aa - bb
    alpha0 = aa / curve
    keep = -bb / curve
    rz1 = keep * keep * aa + 2.0 * keep * alpha0 * bb + alpha0 * alpha0 * cc
    scale = keep + rz1 / aa
    alpha1 = rz1 / (scale * scale * curve + 2.0 * scale * alpha0 * (bb - cc) + alpha0 * alpha0 * dd)
    dir_last = scale * dir0 + alpha0 * dir1
    img_last = scale * image0 + alpha0 * image1
    sol = alpha0 * dir0 + alpha1 * dir_last
    res = keep * res0 + alpha0 * rest - alpha1 * img_last

    def to_rows(value):
        rows = jnp.concatenate([value, jnp.zeros((128, 112), F32)], axis=1).T[:16]
        rows = jnp.concatenate([rows[column_of(j) : column_of(j) + 1] for j in range(9)], axis=0)
        return rows[:, 64 : 64 + OWN]

    sol_ref[...] = to_rows(sol)
    res_ref[...] = to_rows(res)
    sent(v_copies + [first_swap])
    gather_sent(first_msg, 0)


def deliver(sol_in, res_in, sol_out, res_out, sems):
    copies = [
        pltpu.make_async_copy(src, dst, sems.at[i])
        for i, (src, dst) in enumerate(((sol_in, sol_out), (res_in, res_out)))
    ]
    for copy in copies:
        copy.start()
    for copy in copies:
        copy.wait()


def local(jac_cam, jac_point, point_ids, block_cam, block_fill, rhs):
    dma = pltpu.SemaphoreType.DMA
    vmem = pl.BlockSpec(memory_space=pltpu.VMEM)
    hbm = pl.BlockSpec(memory_space=pltpu.HBM)
    own = jax.ShapeDtypeStruct((9, OWN), F32)
    outputs = pl.pallas_call(
        kernel,
        out_shape=(own, own),
        in_specs=[hbm] * 6,
        out_specs=(vmem, vmem),
        scratch_shapes=[
            pltpu.VMEM((18, BLK, SLOTS), F32),
            pltpu.VMEM((6, BLK, SLOTS), F32),
            pltpu.VMEM((BLK, SLOTS), jnp.int32),
            pltpu.VMEM((1, BLK), jnp.int32),
            pltpu.VMEM((1, BLK), jnp.int32),
            pltpu.VMEM((9, OWN), F32),
            pltpu.VMEM((CHUNKS, LO, CHUNK), BF16),
            pltpu.VMEM((CHUNKS, LO, CHUNK), F32),
            pltpu.VMEM((CHUNKS, HI, CHUNK), BF16),
            pltpu.VMEM((2, GROUPS, 128, GROUP * 128), BF16),
            pltpu.VMEM((3, BLK, SLOTS), F32),
            pltpu.VMEM((3, BLK, SLOTS), F32),
            pltpu.VMEM((2, BLK, SLOTS), F32),
            pltpu.VMEM((NCAM, 6 * LQ, HI), F32),
            pltpu.VMEM((NCAM - 1, 6 * LQ, HI), F32),
            pltpu.VMEM((6, LQ, HI), F32),
            pltpu.VMEM((2, NCAM, 3 * LQ, HI), F32),
            pltpu.VMEM((2, NCAM - 1, 3 * LQ, HI), F32),
            pltpu.VMEM((2, NCAM, 3 * LQ, HI), F32),
            pltpu.VMEM((2 * NCAM * 3 * LQ, HI), BF16),
            pltpu.VMEM((2, NCHIP, 2 * MSG, 128), F32),
            pltpu.VMEM((2, 2, NCHIP, MSG, 128), F32),
            pltpu.VMEM((2, NCAM, 1, 128), F32),
            pltpu.VMEM((128, 16), F32),
            pltpu.VMEM((3, 128, 16), F32),
            pltpu.VMEM((2, 128, 16), F32),
            pltpu.VMEM((1, 128), F32),
            dma((6,)),
            dma((3,)),
            dma((3,)),
            dma((3,)),
            dma((3,)),
            dma((NCAM - 1,)),
            dma((NCAM - 1,)),
            dma((2, NCAM - 1)),
            dma((2, NCAM - 1)),
            dma((2, NCAM - 1)),
            dma((2, NCAM - 1)),
            dma((2, NCAM - 1)),
            dma((2, NCAM - 1)),
        ],
        compiler_params=pltpu.CompilerParams(
            collective_id=0, has_side_effects=True, vmem_limit_bytes=60 * 1024 * 1024
        ),
        name="schur_cg",
    )(jac_cam, jac_point, point_ids, block_cam.reshape(1, BLK), block_fill.reshape(1, BLK), rhs)
    return pl.pallas_call(
        deliver,
        out_shape=(own, own),
        in_specs=[vmem] * 2,
        out_specs=(hbm, hbm),
        scratch_shapes=[dma((2,))],
        name="deliver",
    )(*outputs)


def solution(mesh):
    placed = (
        P(None, ("slab", "cam"), None),
        P(None, ("slab", "cam"), None),
        P(("slab", "cam"), None),
        P(("slab", "cam")),
        P(("slab", "cam")),
        P(None, ("slab", "cam")),
    )
    return jax.shard_map(
        local,
        mesh=mesh,
        in_specs=placed,
        out_specs=(P(None, ("slab", "cam")), P(None, ("slab", "cam"))),
        check_vma=False,
    )
```

```python
import jax
import jax.numpy as jnp
from jax import lax
from jax.experimental import pallas as pl
from jax.experimental.pallas import tpu as pltpu
from jax.sharding import PartitionSpec as P

MU = 1.0
LAMBDA = 0.5

MESH = pl.DeviceIdType.MESH
F32 = jnp.float32
BF16 = jnp.bfloat16

BLK = 64
SLOTS = 128
ITERS = 2
OWN = 48
NX = 4
NZ = 8
NCHIP = NX * NZ
NCAM = 4
HI = 256
LO = 64
LQ = LO // NCAM
CHUNK = 256
CHUNKS = BLK * SLOTS // CHUNK
STEPS_V = 8
STEPS_Q = 32
STEPS_W = 16
MSG = 5
GROUP = 4
GROUPS = NCHIP // (2 * GROUP)

NT = (((1,), (1,)), ((), ()))


def dot_nt(a, b):
    return lax.dot_general(a, b, NT, preferred_element_type=F32)


def dot_nn(a, b):
    return lax.dot_general(a, b, (((1,), (0,)), ((), ())), preferred_element_type=F32)


def split2(v):
    hi = v.astype(BF16).astype(F32)
    return hi, v - hi


def split3(v):
    hi, rest = split2(v)
    mid, low = split2(rest)
    return hi, mid, low


def far_first():
    def hops(offset):
        dx, dz = offset
        return min(dx, NX - dx) + min(dz, NZ - dz)

    offsets = [(dx, dz) for dx in range(NX) for dz in range(NZ) if dx or dz]
    return sorted(offsets, key=hops, reverse=True)


OFFSETS = far_first()


def column_of(j):
    return (j % 2) * 8 + j // 2


def total(v):
    return jnp.sum(jnp.sum(v, axis=0, keepdims=True), axis=1, keepdims=True)


def kernel(
    jc_hbm, jp_hbm, pid_hbm, cam_hbm, fill_hbm, rhs_hbm, sol_ref, res_ref,
    jcm, jpm, pid_ref, cam_ref, fill_ref, rhs_ref, low_b, low_f, high, equal, holds, t_ref, w_obs, e_ref,
    v_part, v_recv, vinv, q_part, q_recv, w_full, w_split, first_msg, msgs, sc,
    precond_ref, vecs, images, dots_ref, ins, cs, cr, ps, pr, vs, vr, qs, qr, ws, wr, ss, sr,
):
    slab = lax.axis_index("slab")
    cam = lax.axis_index("cam")
    core = lax.rem(slab, 2)
    z = lax.rem(lax.div(slab, 2), NZ)
    x = lax.div(slab, 2 * NZ)
    chip = x * NZ + z

    def chip_peer(offset):
        dx, dz = offset
        other = lax.rem(x + dx, NX) * NZ + lax.rem(z + dz, NZ)
        return (other * 2 + core, cam)

    sibling = (chip * 2 + (1 - core), cam)

    def cam_peer(d):
        return (slab, lax.rem(cam + d, NCAM))

    barrier = pltpu.get_barrier_semaphore()
    for offset in OFFSETS:
        pl.semaphore_signal(barrier, inc=1, device_id=chip_peer(offset), device_id_type=MESH)
    for d in range(1, NCAM):
        pl.semaphore_signal(barrier, inc=1, device_id=cam_peer(d), device_id_type=MESH)
    pl.semaphore_signal(barrier, inc=1, device_id=sibling, device_id_type=MESH)

    inputs = [
        pltpu.make_async_copy(src, dst, ins.at[i])
        for i, (src, dst) in enumerate(
            (
                (fill_hbm, fill_ref), (cam_hbm, cam_ref), (rhs_hbm, rhs_ref),
                (jc_hbm, jcm), (pid_hbm, pid_ref), (jp_hbm, jpm),
            )
        )
    ]
    for copy in inputs:
        copy.start()
    def remote(src, dst, send, recv, device):
        copy = pltpu.make_async_remote_copy(
            src_ref=src, dst_ref=dst, send_sem=send, recv_sem=recv, device_id=device, device_id_type=MESH
        )
        copy.start()
        return copy

    def received(ref, send, recv, device):
        return pltpu.make_async_remote_copy(
            src_ref=ref, dst_ref=ref, send_sem=send, recv_sem=recv, device_id=device, device_id_type=MESH
        )

    def wait_all(copies):
        for copy in copies:
            copy.wait_recv()

    def sent(copies):
        for copy in copies:
            copy.wait_send()

    last = NCHIP - 1

    def gather_start(buf, m):
        for i, offset in enumerate(OFFSETS):
            remote(buf.at[core, last], buf.at[core, i], cs.at[m], cr.at[m], chip_peer(offset))

    def gather_middle(buf, m):
        others = buf.at[core, pl.ds(0, last)]
        received(others, cs.at[m], cr.at[m], sibling).wait_recv()
        return remote(buf.at[core], buf.at[core], ps.at[m], pr.at[m], sibling)

    def gather_sent(buf, m):
        others = buf.at[core, pl.ds(0, last)]
        received(others, cs.at[m], cr.at[m], sibling).wait_send()

    lane8 = lax.broadcasted_iota(jnp.int32, (8, 128), 1)

    def side_by_side(first, second):
        first, second = [
            jnp.concatenate([v, jnp.zeros((8 - MSG, 128), F32)], axis=0) for v in (first, second)
        ]
        even = jnp.where(lane8 < 64, first, pltpu.roll(second, 64, 1))
        odd = jnp.where(lane8 < 64, pltpu.roll(first, 64, 1), second)
        return jnp.concatenate([even, odd], axis=0)

    def camera_sums(read, matrix, acc, of_core):
        for group in range(GROUPS):
            slots = range(2 * GROUP * group, 2 * GROUP * (group + 1), 2)
            wide = jnp.concatenate(
                [side_by_side(read(of_core, slot), read(of_core, slot + 1)) for slot in slots], axis=1
            )
            parts = jnp.concatenate(split3(wide), axis=0).astype(BF16)
            acc = acc + dot_nt(matrix(of_core, group), parts)
        return acc

    zero_sums = jnp.zeros((128, 48), F32)

    def three_parts(acc):
        return acc[:, 0:16] + acc[:, 16:32] + acc[:, 32:48]

    def column(row):
        wide = jnp.concatenate([row, jnp.zeros((1, 64), F32)], axis=1)
        return jnp.broadcast_to(wide, (128, 128)).T

    for copy in inputs[:4]:
        copy.wait()
    cam_col = column(cam_ref[...].astype(F32))
    fill_col = column(fill_ref[...].astype(F32))
    sub = lax.broadcasted_iota(jnp.int32, (128, 128), 0)
    lane = lax.broadcasted_iota(jnp.int32, (128, 128), 1)
    own_cam = (slab * OWN + sub - 64).astype(F32)
    is_own = (sub >= 64) & (sub < 64 + OWN)
    targets = jnp.where(sub < 64, cam_col, jnp.where(is_own, own_cam, -1.0))

    live = (lane.astype(F32) < fill_col)[:BLK]
    for i in range(18):
        jcm[i] = jnp.where(live, jcm[i], 0.0)

    lane64 = lane[:BLK]
    sub64 = sub[:BLK]

    def spread(values):
        halves = []
        for rest in range(2):
            half = jnp.zeros((BLK, 128), F32)
            for j in range(rest, 9, 2):
                half = jnp.where(lane64 == j // 2, values[j], half)
            halves.append(half)
        return halves

    def message(even, odd):
        return jnp.concatenate([even, odd], axis=0).T[:MSG]

    even, odd = spread(
        [jnp.sum(jcm[j] * jcm[j] + jcm[9 + j] * jcm[9 + j], axis=1, keepdims=True) for j in range(9)]
    )
    odd = jnp.where(lane64 == 4, cam_col[:BLK], odd)
    rhs = rhs_ref[...]
    gap = jnp.zeros((MSG, 64 - OWN), F32)
    none = jnp.zeros((1, OWN), F32)
    rhs_even = jnp.concatenate([rhs[j : j + 1] for j in range(0, 9, 2)], axis=0)
    rhs_odd = jnp.concatenate([rhs[j : j + 1] for j in range(1, 9, 2)] + [none], axis=0)
    first_msg[core, last] = jnp.concatenate(
        [message(even, odd), jnp.concatenate([rhs_even, gap, rhs_odd, gap], axis=1)], axis=0
    )

    inputs[4].wait()

    def build(k, carry):
        ids = jnp.concatenate([pid_ref[pl.ds(2 * k, 1), :], pid_ref[pl.ds(2 * k + 1, 1), :]], axis=1)
        low = lax.bitwise_and(ids, LO - 1)
        top = lax.shift_right_logical(ids, 6)
        hot = lax.broadcasted_iota(jnp.int32, (HI, CHUNK), 0) == top
        high[k] = jnp.where(hot, 1.0, 0.0).astype(BF16)
        hot_low = jnp.where(lax.broadcasted_iota(jnp.int32, (LO, CHUNK), 0) == low, 1.0, 0.0)
        low_f[k] = hot_low
        low_b[k] = hot_low.astype(BF16)
        return carry

    lax.fori_loop(0, CHUNKS, build, 0)
    inputs[5].wait()
    for i in range(6):
        jpm[i] = jnp.where(live, jpm[i], 0.0)

    pl.semaphore_wait(barrier, len(OFFSETS) + NCAM)
    gather_start(first_msg, 0)
    lane1 = lax.broadcasted_iota(jnp.int32, (1, 128), 1)

    def owner_matrix(of_core, group):
        place = lax.rem(lane1, 64)
        blocks = []
        for p in range(GROUP):
            slot = 2 * (GROUP * group + p)
            first, second = [
                lax.rem(x - dx + NX, NX) * NZ + lax.rem(z - dz + NZ, NZ)
                for dx, dz in (OFFSETS + [(0, 0)])[slot : slot + 2]
            ]
            source = jnp.where(lane1 < 64, first, second) * 2 + of_core
            ids = jnp.where(place < OWN, source * OWN + place, -2).astype(F32)
            blocks.append(jnp.where(targets == ids, 1.0, 0.0).astype(BF16))
        return jnp.concatenate(blocks, axis=1)

    for of_core in range(2):
        for group in range(GROUPS):
            holds[of_core, group] = owner_matrix(of_core, group)

    def pair(ref, index, k):
        return jnp.concatenate([ref[index, pl.ds(2 * k, 1), :], ref[index, pl.ds(2 * k + 1, 1), :]], axis=1)

    def scatter(rows_of, count, acc_ref, steps):
        half = NCAM * count * LQ
        acc_ref[...] = jnp.zeros_like(acc_ref)

        def body(step, carry):
            summed = None
            for u in range(steps):
                k = step * steps + u
                parts = [], []
                for row in rows_of(k):
                    for part, value in zip(parts, split2(row)):
                        part.append(jnp.broadcast_to(value, (LQ, CHUNK)).astype(BF16))
                blocks = [
                    low_b[k, LQ * q : LQ * (q + 1), :] * value
                    for part in parts
                    for q in range(NCAM)
                    for value in part
                ]
                product = dot_nt(jnp.concatenate(blocks, axis=0), high[k])
                summed = product if summed is None else summed + product
            acc_ref[...] += (summed[:half] + summed[half:]).reshape(NCAM, count * LQ, HI)
            return carry

        lax.fori_loop(0, CHUNKS // steps, body, 0)

    def jp_products(k):
        a = [pair(jpm, i, k) for i in range(6)]
        return [a[i] * a[j] + a[3 + i] * a[3 + j] for i, j in ((0, 0), (0, 1), (0, 2), (1, 1), (1, 2), (2, 2))]

    scatter(jp_products, 6, v_part, STEPS_V)
    first_swap = gather_middle(first_msg, 0)
    v_copies = [
        remote(v_part.at[lax.rem(cam + d, NCAM)], v_recv.at[d - 1], vs.at[d - 1], vr.at[d - 1], cam_peer(d))
        for d in range(1, NCAM)
    ]


    def same(of_core, group):
        blocks = []
        for p in range(GROUP):
            slot = 2 * (GROUP * group + p)
            first, second = [first_msg[of_core, slot + i, MSG - 1 : MSG, :] for i in range(2)]
            ids = jnp.where(lane1 < 64, pltpu.roll(first, 64, 1), second)
            blocks.append(jnp.where(targets == ids, 1.0, 0.0).astype(BF16))
        matrix = jnp.concatenate(blocks, axis=1)
        equal[of_core, group] = matrix
        return matrix

    def owned(of_core, group):
        return holds[of_core, group]

    def saved(of_core, group):
        return equal[of_core, group]

    lane16 = lax.broadcasted_iota(jnp.int32, (128, 16), 1)
    sub16 = lax.broadcasted_iota(jnp.int32, (128, 16), 0)
    param = (lane16 < 5) | ((lane16 >= 8) & (lane16 < 12))
    mine = param & (sub16 >= 64) & (sub16 < 64 + OWN)

    def read_first(at):
        return lambda of_core, slot: first_msg[of_core, slot, MSG * at : MSG * (at + 1), :]

    diag_sums = camera_sums(read_first(0), same, zero_sums, core)
    rhs_sums = camera_sums(read_first(1), owned, zero_sums, core)
    first_swap.wait_recv()
    diag_sums = camera_sums(read_first(0), same, diag_sums, 1 - core)
    rhs_sums = camera_sums(read_first(1), owned, rhs_sums, 1 - core)
    precond = jnp.where(param, three_parts(diag_sums), 0.0) + LAMBDA
    res0 = three_parts(rhs_sums)
    precond_ref[...] = precond
    vecs[0] = res0 / precond
    vecs[1] = res0
    dots_ref[...] = jnp.zeros((1, 128), F32)

    def apply(it, carry):
        vec = vecs[it]
        cols = [jnp.broadcast_to(vec[:BLK, column_of(j) : column_of(j) + 1], (BLK, SLOTS)) for j in range(9)]
        for r in range(2):
            e = jcm[9 * r] * cols[0]
            for j in range(1, 9):
                e = e + jcm[9 * r + j] * cols[j]
            e_ref[r] = e
        for a in range(3):
            t_ref[a] = jpm[a] * e_ref[0] + jpm[3 + a] * e_ref[1]
        scatter(lambda k: [pair(t_ref, a, k) for a in range(3)], 3, q_part.at[it], STEPS_Q)
        q_copies = [
            remote(
                q_part.at[it, lax.rem(cam + d, NCAM)], q_recv.at[it, d - 1],
                qs.at[it, d - 1], qr.at[it, d - 1], cam_peer(d),
            )
            for d in (2, 1, 3)
        ]
        square = LAMBDA * total(jnp.where(mine, vec * vec, 0.0))
        square = square + total(e_ref[0] * e_ref[0] + e_ref[1] * e_ref[1])

        @pl.when(it == 0)
        def invert():
            wait_all(v_copies)
            v = v_part[cam] + v_recv[0] + v_recv[1] + v_recv[2]
            v00, v01, v02, v11, v12, v22 = [v[LQ * i : LQ * (i + 1)] for i in range(6)]
            v00, v11, v22 = v00 + MU, v11 + MU, v22 + MU
            c00 = v11 * v22 - v12 * v12
            c01 = v02 * v12 - v01 * v22
            c02 = v01 * v12 - v02 * v11
            c11 = v00 * v22 - v02 * v02
            c12 = v01 * v02 - v00 * v12
            c22 = v00 * v11 - v01 * v01
            det = v00 * c00 + v01 * c01 + v02 * c02
            for i, value in enumerate((c00, c01, c02, c11, c12, c22)):
                vinv[i] = value / det

        wait_all(q_copies)
        q = q_part[it, cam] + q_recv[it, 0] + q_recv[it, 1] + q_recv[it, 2]
        q0, q1, q2 = [q[LQ * i : LQ * (i + 1)] for i in range(3)]
        w0 = vinv[0] * q0 + vinv[1] * q1 + vinv[2] * q2
        w1 = vinv[1] * q0 + vinv[3] * q1 + vinv[4] * q2
        w2 = vinv[2] * q0 + vinv[4] * q1 + vinv[5] * q2
        w_full[it, cam] = jnp.concatenate([w0, w1, w2], axis=0)
        w_copies = [
            remote(w_full.at[it, cam], w_full.at[it, cam], ws.at[it, d - 1], wr.at[it, d - 1], cam_peer(d))
            for d in (2, 1, 3)
        ]
        square = square - total(q0 * w0 + q1 * w1 + q2 * w2)
        sc[it, cam] = jnp.where(lane1 == 3, square, dots_ref[...])
        sc_copies = [
            remote(sc.at[it, cam], sc.at[it, cam], ss.at[it, d - 1], sr.at[it, d - 1], cam_peer(d))
            for d in (2, 1, 3)
        ]
        half = NCAM * 3 * LQ

        def keep_split(peer):
            for part, value in enumerate(split2(w_full[it, peer])):
                w_split[part, peer] = value.astype(BF16)

        keep_split(cam)
        for copy, d in ((w_copies[1], 1), (w_copies[2], 3), (w_copies[0], 2)):
            copy.wait_recv()
            keep_split(lax.rem(cam + NCAM - d, NCAM))

        def body(step, carry):
            for u in range(STEPS_W):
                k = step * STEPS_W + u
                product = dot_nn(w_split[...].reshape(2 * half, HI), high[k])
                product = product[:half] + product[half:]
                for c in range(3):
                    picked = jnp.zeros((LQ, CHUNK), F32)
                    for q in range(NCAM):
                        at = (3 * q + c) * LQ
                        picked = picked + product[at : at + LQ] * low_f[k, LQ * q : LQ * (q + 1), :]
                    row = jnp.sum(picked, axis=0, keepdims=True)
                    w_obs[c, pl.ds(2 * k, 1), :] = row[:, :SLOTS]
                    w_obs[c, pl.ds(2 * k + 1, 1), :] = row[:, SLOTS:]
            return carry

        lax.fori_loop(0, CHUNKS // STEPS_W, body, 0)
        d = [
            e_ref[r] - (jpm[3 * r] * w_obs[0] + jpm[3 * r + 1] * w_obs[1] + jpm[3 * r + 2] * w_obs[2])
            for r in range(2)
        ]
        even, odd = spread(
            [jnp.sum(jcm[j] * d[0] + jcm[9 + j] * d[1], axis=1, keepdims=True) for j in range(9)]
        )
        wait_all(sc_copies)
        sums = pltpu.roll(sc[it, 0] + sc[it, 1] + sc[it, 2] + sc[it, 3], 64, 1)
        buf = msgs.at[it]
        terms = message(even, odd)
        extra = jnp.where((lane1 >= 64) & (lane1 < 68), sums, terms[MSG - 1 :])
        buf[core, last] = jnp.concatenate([terms[: MSG - 1], extra], axis=0)
        gather_start(buf, 1 + it)
        sent(q_copies + w_copies + sc_copies)
        swap = gather_middle(buf, 1 + it)

        def read(of_core, slot):
            return msgs[it, of_core, slot]

        acc = camera_sums(read, saved, zero_sums, core)
        swap.wait_recv()
        acc = camera_sums(read, saved, acc, 1 - core)
        image = jnp.where(param, three_parts(acc), 0.0) + LAMBDA * vec
        images[it] = image

        @pl.when(it == 0)
        def prepare():
            res0 = vecs[1]
            rest = res0 - image
            following = rest / precond_ref[...]
            row = jnp.zeros((1, 128), F32)
            for i, (a, b) in enumerate(((res0, vec), (vec, rest), (rest, following))):
                row = jnp.where(lane1 == i, total(jnp.where(mine, a * b, 0.0)), row)
            dots_ref[...] = row
            vecs[1] = following
            vecs[2] = res0

        swap.wait_send()
        gather_sent(buf, 1 + it)
        return carry

    lax.fori_loop(0, ITERS, apply, 0)
    dir0, dir1, res0 = vecs[0], vecs[1], vecs[2]
    image0, image1 = images[0], images[1]
    rest = res0 - image0
    sums = jnp.sum(msgs[1, 0] + msgs[1, 1], axis=0)[MSG - 1 : MSG]
    aa, bb, cc, dd = [sums[:, 64 + i : 65 + i] for i in range(4)]
    curve = aa - bb
    alpha0 = aa / curve
    keep = -bb / curve
    rz1 = keep * keep * aa + 2.0 * keep * alpha0 * bb + alpha0 * alpha0 * cc
    scale = keep + rz1 / aa
    alpha1 = rz1 / (scale * scale * curve + 2.0 * scale * alpha0 * (bb - cc) + alpha0 * alpha0 * dd)
    dir_last = scale * dir0 + alpha0 * dir1
    img_last = scale * image0 + alpha0 * image1
    sol = alpha0 * dir0 + alpha1 * dir_last
    res = keep * res0 + alpha0 * rest - alpha1 * img_last

    both = jnp.concatenate([sol, res, jnp.zeros((128, 96), F32)], axis=1).T
    for at, out in ((0, sol_ref), (16, res_ref)):
        rows = jnp.concatenate([both[at + column_of(j) : at + column_of(j) + 1] for j in range(9)], axis=0)
        out[...] = rows[:, 64 : 64 + OWN]
    sent(v_copies + [first_swap])
    gather_sent(first_msg, 0)


def deliver(sol_in, res_in, sol_out, res_out, sems):
    copies = [
        pltpu.make_async_copy(src, dst, sems.at[i])
        for i, (src, dst) in enumerate(((sol_in, sol_out), (res_in, res_out)))
    ]
    for copy in copies:
        copy.start()
    for copy in copies:
        copy.wait()


def local(jac_cam, jac_point, point_ids, block_cam, block_fill, rhs):
    dma = pltpu.SemaphoreType.DMA
    vmem = pl.BlockSpec(memory_space=pltpu.VMEM)
    hbm = pl.BlockSpec(memory_space=pltpu.HBM)
    own = jax.ShapeDtypeStruct((9, OWN), F32)
    outputs = pl.pallas_call(
        kernel,
        out_shape=(own, own),
        in_specs=[hbm] * 6,
        out_specs=(vmem, vmem),
        scratch_shapes=[
            pltpu.VMEM((18, BLK, SLOTS), F32),
            pltpu.VMEM((6, BLK, SLOTS), F32),
            pltpu.VMEM((BLK, SLOTS), jnp.int32),
            pltpu.VMEM((1, BLK), jnp.int32),
            pltpu.VMEM((1, BLK), jnp.int32),
            pltpu.VMEM((9, OWN), F32),
            pltpu.VMEM((CHUNKS, LO, CHUNK), BF16),
            pltpu.VMEM((CHUNKS, LO, CHUNK), F32),
            pltpu.VMEM((CHUNKS, HI, CHUNK), BF16),
            pltpu.VMEM((2, GROUPS, 128, GROUP * 128), BF16),
            pltpu.VMEM((2, GROUPS, 128, GROUP * 128), BF16),
            pltpu.VMEM((3, BLK, SLOTS), F32),
            pltpu.VMEM((3, BLK, SLOTS), F32),
            pltpu.VMEM((2, BLK, SLOTS), F32),
            pltpu.VMEM((NCAM, 6 * LQ, HI), F32),
            pltpu.VMEM((NCAM - 1, 6 * LQ, HI), F32),
            pltpu.VMEM((6, LQ, HI), F32),
            pltpu.VMEM((2, NCAM, 3 * LQ, HI), F32),
            pltpu.VMEM((2, NCAM - 1, 3 * LQ, HI), F32),
            pltpu.VMEM((2, NCAM, 3 * LQ, HI), F32),
            pltpu.VMEM((2, NCAM, 3 * LQ, HI), BF16),
            pltpu.VMEM((2, NCHIP, 2 * MSG, 128), F32),
            pltpu.VMEM((2, 2, NCHIP, MSG, 128), F32),
            pltpu.VMEM((2, NCAM, 1, 128), F32),
            pltpu.VMEM((128, 16), F32),
            pltpu.VMEM((3, 128, 16), F32),
            pltpu.VMEM((2, 128, 16), F32),
            pltpu.VMEM((1, 128), F32),
            dma((6,)),
            dma((3,)),
            dma((3,)),
            dma((3,)),
            dma((3,)),
            dma((NCAM - 1,)),
            dma((NCAM - 1,)),
            dma((2, NCAM - 1)),
            dma((2, NCAM - 1)),
            dma((2, NCAM - 1)),
            dma((2, NCAM - 1)),
            dma((2, NCAM - 1)),
            dma((2, NCAM - 1)),
        ],
        compiler_params=pltpu.CompilerParams(
            collective_id=0, has_side_effects=True, vmem_limit_bytes=60 * 1024 * 1024
        ),
        name="schur_cg",
    )(jac_cam, jac_point, point_ids, block_cam.reshape(1, BLK), block_fill.reshape(1, BLK), rhs)
    return pl.pallas_call(
        deliver,
        out_shape=(own, own),
        in_specs=[vmem] * 2,
        out_specs=(hbm, hbm),
        scratch_shapes=[dma((2,))],
        name="deliver",
    )(*outputs)


def solution(mesh):
    placed = (
        P(None, ("slab", "cam"), None),
        P(None, ("slab", "cam"), None),
        P(("slab", "cam"), None),
        P(("slab", "cam")),
        P(("slab", "cam")),
        P(None, ("slab", "cam")),
    )
    return jax.shard_map(
        local,
        mesh=mesh,
        in_specs=placed,
        out_specs=(P(None, ("slab", "cam")), P(None, ("slab", "cam"))),
        check_vma=False,
    )
```
